32 devices in a mesh: groups: 2 (over y), dp: 4 (over z), tp: 4 (over x, core).
Axes of the slice: x: 2, y: 2, z: 4, core: 2. Of those that a mesh axis runs over, the one named last changes fastest.
Arguments:
- hidden: bfloat16 [4096, 3584], P(('groups', 'dp')), parts along dimension 0, may hold values from -24 to 24
- lengths: int32 [8, 32], P(('groups', 'dp')), parts along dimension 0, may hold values from 1 to 128, 512 in all within a row
- list_ids: int32 [8, 32], P(('groups', 'dp')), parts along dimension 0, may hold values from 0 to 31, as said below
- list_slot: int32 [64], P('groups'), parts along dimension 0, may hold values from 0 to 31, as said below
- gain: float32 [3584], replicated, may hold values from 0.1 to 1.9
- w_query: bfloat16 [3584, 2048], P('dp', 'tp'), may hold values from -0.09375 to 0.09375
- b_query: bfloat16 [2048], P('tp'), may hold values from -100 to 100
- w_keyval: bfloat16 [3584, 1024], P('dp', 'tp'), may hold values from -0.09375 to 0.09375
- b_keyval: bfloat16 [1024], replicated, may hold values from -6 to 6
- w_out: bfloat16 [2048, 3584], P('tp', 'dp'), may hold values from -0.125 to 0.125
- w_pool: bfloat16 [3584, 1024], P('tp'), may hold values from -0.09375 to 0.09375
- centroids: float32 [32, 1024], P('dp', 'tp'), may hold values from -5 to 5
Outputs:
- layer_out: bfloat16 [4096, 3584], P(('groups', 'dp'), 'tp'), parts along dimension 0
- residual_sums: float32 [64, 1024], P(('groups', 'dp'), 'tp'), parts along dimension 0
- list_counts: int32 [64], P(('groups', 'dp')), parts along dimension 0
The draws below stay inside these ranges and needn't reach their ends.
There are 2 independent parts, one for each index of `groups`. The reference program is written for one: setup_inputs(seed, part) draws one part's arguments, and reference() takes and returns one part's arrays. A program takes and returns all parts, laid end to end along the dimension named above; an argument that names none is the same for every part. Nothing has to cross between parts.
Inputs may be any that keep to these rules, and one draw needn't show every extreme that they name: List l is owned by index list_slot[l] // 8 of dp; list_slot is a permutation. `list_ids`: the captions of one index of dp go to at most 16 captions for any one owner; in every draw some owner gets exactly 16 from every index of dp.
All inputs are finite; a program needn't handle non-finite values.
Results may differ from the reference program's by a relative error of at most 0.009.
Values may be sent and summed in bfloat16 or wider, within the bound.
No kernel may reach another device: no remote copies, remote signals or barrier semaphores. Data moves between devices by JAX's collectives and lax.ppermute only.
A program may use at most 128 MiB of HBM per device.

```python
import math
import jax
import jax.numpy as jnp
import numpy as np
from jax import lax

D = 3584
KV_HEADS = 4
HD = 128
Q_HEADS = 16
E = 1024
LISTS_DEV = 8
TOK_DEV = 512
CAP_DEV = 32
TOKENS = 2048
LISTS = 32
SEND_CAP = 16
N_DP = 4
N_TP = 4


def owner_plan(key):
    top = jax.random.randint(jax.random.fold_in(key, 11), (), 0, N_DP)

    def one_device(index):
        device_key = jax.random.fold_in(jax.random.fold_in(key, 12), index)
        order = jax.random.permutation(jax.random.fold_in(device_key, 1), (N_DP - 1) * SEND_CAP)
        others = ((top + 1 + order // SEND_CAP) % N_DP).astype(jnp.int32)
        owners = jnp.concatenate([jnp.full((SEND_CAP,), top, dtype=jnp.int32), others[:CAP_DEV - SEND_CAP]])
        shuffle = jax.random.permutation(jax.random.fold_in(device_key, 2), CAP_DEV)
        owners = owners[shuffle]
        local = jax.random.randint(jax.random.fold_in(device_key, 3), (CAP_DEV,), 0, LISTS_DEV)
        return (owners * LISTS_DEV + local).astype(jnp.int32)
    slots = jax.vmap(one_device)(jnp.arange(N_DP, dtype=jnp.int32))
    slot_of_list = jax.random.permutation(jax.random.fold_in(key, 13), LISTS).astype(jnp.int32)
    list_of_slot = jnp.argsort(slot_of_list, stable=True).astype(jnp.int32)
    return (list_of_slot[slots], slot_of_list)


def bias_direction(key):
    return jnp.clip(jax.random.normal(jax.random.fold_in(key, 21), (KV_HEADS, HD), jnp.float32), -3.0, 3.0)


def draw_list_ids(key, part):
    chosen, mapping = owner_plan(key)
    return chosen


def draw_list_slot(key, part):
    chosen, mapping = owner_plan(key)
    return mapping


def draw_hidden(key, part):
    key = jax.random.fold_in(key, 1)
    first, second, third = jax.random.split(key, 3)
    row_scale = jnp.exp(jax.random.uniform(first, (TOKENS, 1), jnp.float32, jnp.log(0.3), jnp.log(3.0)))
    col_scale = jnp.exp(jax.random.uniform(second, (1, D), jnp.float32, jnp.log(0.5), jnp.log(2.0)))
    base = jnp.clip(jax.random.normal(third, (TOKENS, D), jnp.float32), -4.0, 4.0)
    return (base * row_scale * col_scale).astype(jnp.bfloat16)


def draw_b_query(key, part):
    direction = bias_direction(key)
    key = jax.random.fold_in(key, 2)
    first = jax.random.fold_in(key, 0)
    fourth = jax.random.fold_in(key, 3)
    weak = jax.random.uniform(first, (Q_HEADS,), jnp.float32, -0.3, 0.3)
    strength = weak
    owner_head = jnp.arange(Q_HEADS) // (Q_HEADS // KV_HEADS)
    noise = jnp.clip(0.5 * jax.random.normal(fourth, (Q_HEADS, HD), jnp.float32), -2.0, 2.0)
    bias = strength[:, None] * direction[owner_head] + noise
    return bias.reshape(Q_HEADS * HD).astype(jnp.bfloat16)


def draw_b_keyval(key, part):
    direction = bias_direction(key)
    key = jax.random.fold_in(key, 3)
    first, second = jax.random.split(key, 2)
    key_part = direction + jnp.clip(0.3 * jax.random.normal(first, (KV_HEADS, HD), jnp.float32), -1.2, 1.2)
    value_part = jnp.clip(0.5 * jax.random.normal(second, (KV_HEADS, HD), jnp.float32), -2.0, 2.0)
    return jnp.concatenate([key_part.reshape(-1), value_part.reshape(-1)]).astype(jnp.bfloat16)


def steps_of(rng, dims, pieces, smallest, high):
    factor_of, own = 1.0, jax.random.fold_in(rng, 6)
    for axis_at, parts in pieces:
        steps = jnp.exp(jax.random.uniform(jax.random.fold_in(own, axis_at), (parts,), jnp.float32, smallest / len(pieces), high / len(pieces)))
        factor_of = factor_of * jnp.repeat(steps, dims[axis_at] // parts).reshape([-1 if axis == axis_at else 1 for axis in range(len(dims))])
    return factor_of


def profile(count, total, limit, skew):
    loads = [(1 << 20) // math.isqrt(standing ** skew) + 1 for standing in range(2, count + 1)]
    rest, counts = total - limit - (count - 1), [1] * (count - 1)
    while rest > 0:
        movable = [i for i in range(count - 1) if counts[i] < limit]
        whole, left = sum([loads[i] for i in movable]), rest
        for i in movable:
            extra = min(limit - counts[i], max(1, left * loads[i] // whole), rest)
            counts[i] = counts[i] + extra
            rest = rest - extra
    return np.array([limit] + counts)


def uneven_parts(own_key, amount, total, most, skew):
    if amount == 2:
        one = jax.random.randint(own_key, (), max(1, total - most), min(most, total - 1) + 1)
        return jnp.stack([one, total - one])
    tallies = jnp.asarray(profile(amount, total, most, skew), jnp.int32)
    pairs = (amount - 1) // 2
    donor, taker = tallies[1:1 + 2 * pairs:2], tallies[2:2 + 2 * pairs:2]
    room = jnp.minimum(donor - 1, most - taker)
    passed = jax.random.randint(jax.random.fold_in(own_key, 1), (pairs,), 0, 1 << 20) % (room + 1)
    tallies = tallies.at[1:1 + 2 * pairs:2].set(donor - passed).at[2:2 + 2 * pairs:2].set(taker + passed)
    return tallies[jax.random.permutation(jax.random.fold_in(own_key, 2), amount)]


def normal_values(key, dims, width, limit, pieces=(), kind=jnp.bfloat16):
    drawn = jax.random.normal(key, dims, jnp.float32) * width
    if len(pieces) > 0:
        drawn = steps_of(key, dims, pieces, -0.22, 0.18) * drawn
    return jnp.clip(drawn, min=-limit, max=limit).astype(kind)


def setup_inputs(seed: int = 0, part: int = 0) -> dict:
    seeds = jax.random.split(jax.random.key(seed), 13)
    part_splits = jax.random.split(jax.random.fold_in(seeds[12], part), 13)
    return {
        "hidden": draw_hidden(jax.random.fold_in(jax.random.fold_in(seeds[12], part), 71), part),
        "lengths": jax.vmap(lambda own: uneven_parts(own, CAP_DEV, TOK_DEV, TOK_DEV // 4, 2))(jax.random.split(part_splits[1], N_DP)).reshape((N_DP, CAP_DEV)).astype(jnp.int32),
        "list_ids": draw_list_ids(jax.random.fold_in(jax.random.fold_in(seeds[12], part), 71), part),
        "list_slot": draw_list_slot(jax.random.fold_in(jax.random.fold_in(seeds[12], part), 71), part),
        "gain": jnp.clip(1.0 + 0.18 * jax.random.normal(seeds[4], (D,), jnp.float32), 0.1, 1.9),
        "w_query": normal_values(seeds[5], (D, Q_HEADS * HD), D ** -0.5, 0.09375, ((0, 4), (1, 4))),
        "b_query": draw_b_query(jax.random.fold_in(seeds[12], 71), part),
        "w_keyval": normal_values(seeds[7], (D, 2 * KV_HEADS * HD), D ** -0.5, 0.09375, ((0, 4), (1, 4))),
        "b_keyval": draw_b_keyval(jax.random.fold_in(seeds[12], 71), part),
        "w_out": normal_values(seeds[9], (Q_HEADS * HD, D), (Q_HEADS * HD) ** -0.5, 0.125, ((0, 4), (1, 4))),
        "w_pool": normal_values(seeds[10], (D, E), D ** -0.5, 0.09375, ((0, 4),)),
        "centroids": normal_values(seeds[11], (LISTS, E), 1.0, 5.0, ((0, 4), (1, 4)), jnp.float32),
    }


rope_base = 1000000.0

def rotate(values, places):
    half = HD // 2
    freq = rope_base ** (-(2.0 / HD) * jnp.arange(half, dtype=jnp.float32))
    angle = places.astype(jnp.float32)[:, None] * freq[None, :]
    cosine = jnp.cos(angle)[:, None, :]
    sine = jnp.sin(angle)[:, None, :]
    shaped = values.reshape(values.shape[0], -1, HD)
    first = shaped[..., :half]
    second = shaped[..., half:]
    turned = jnp.concatenate([first * cosine - second * sine, second * cosine + first * sine], axis=-1)
    return turned.reshape(values.shape)

def positions_of(lengths_row):
    ends = jnp.cumsum(lengths_row, dtype=jnp.int32)
    index = jnp.arange(TOK_DEV, dtype=jnp.int32)
    segment = lax.optimization_barrier(jnp.sum((index[:, None] >= ends[None, :]).astype(jnp.int32), axis=1, dtype=jnp.int32))
    member = segment[None, :] == jnp.arange(CAP_DEV, dtype=jnp.int32)[:, None]
    starts = ends - lengths_row
    place = index - lax.optimization_barrier(jnp.sum(jnp.where(member, starts[:, None], 0), axis=0, dtype=jnp.int32))
    return (segment, member, place)

def attend(block):
    query, keys, values, segment = block
    count = query.shape[0]
    grouped = query.reshape(count, KV_HEADS, Q_HEADS // KV_HEADS, HD).astype(jnp.float32)
    keyed = keys.reshape(count, KV_HEADS, HD).astype(jnp.float32)
    scores = jnp.einsum('skgd,tkd->kgst', grouped, keyed) * HD ** (-0.5)
    allowed = segment[:, None] == segment[None, :]
    scores = jnp.where(allowed[None, None], scores, -1e+30)
    probs = jax.nn.softmax(scores, axis=-1).astype(jnp.bfloat16)
    mixed = jnp.einsum('kgst,tkd->skgd', probs.astype(jnp.float32), values.reshape(count, KV_HEADS, HD).astype(jnp.float32))
    return mixed.reshape(count, Q_HEADS * HD).astype(jnp.bfloat16)

def reference(hidden, lengths, list_ids, list_slot, gain, w_query, b_query, w_keyval, b_keyval, w_out, w_pool, centroids):
    wide = hidden.astype(jnp.float32)
    normed = (wide * lax.rsqrt(lax.optimization_barrier(jnp.mean(wide * wide, axis=1, keepdims=True)) + 1e-06) * gain.astype(jnp.float32)).astype(jnp.bfloat16)
    segment, member, place = jax.vmap(positions_of)(lengths)
    place = place.reshape(-1)
    query = jnp.dot(normed, w_query, preferred_element_type=jnp.float32) + b_query.astype(jnp.float32)
    query = rotate(query, place).astype(jnp.bfloat16)
    keyval = jnp.dot(normed, w_keyval, preferred_element_type=jnp.float32) + b_keyval.astype(jnp.float32)
    kv_width = KV_HEADS * HD
    keys = rotate(keyval[:, :kv_width], place).astype(jnp.bfloat16)
    values = keyval[:, kv_width:].astype(jnp.bfloat16)
    attn = lax.map(attend, (query.reshape(N_DP, TOK_DEV, -1), keys.reshape(N_DP, TOK_DEV, -1), values.reshape(N_DP, TOK_DEV, -1), segment))
    attn = attn.reshape(TOKENS, Q_HEADS * HD)
    share = Q_HEADS * HD // N_TP
    heads_out = jnp.zeros((TOKENS, D), jnp.float32)
    for group in range(N_TP):
        term = jnp.dot(attn[:, group * share:(group + 1) * share], w_out[group * share:(group + 1) * share], preferred_element_type=jnp.float32)
        term = lax.optimization_barrier(term.astype(jnp.bfloat16))
        heads_out = heads_out + term.astype(jnp.float32)
    layer_out = (wide + heads_out).astype(jnp.bfloat16)
    blocks = layer_out.reshape(N_DP, TOK_DEV, D).astype(jnp.float32)
    pooled = jnp.einsum('bct,btd->bcd', member.astype(jnp.float32), blocks)
    pooled = (pooled / lengths.astype(jnp.float32)[:, :, None]).astype(jnp.bfloat16).reshape(N_DP * CAP_DEV, D)
    vec = jnp.dot(pooled, w_pool, preferred_element_type=jnp.float32).astype(jnp.bfloat16)
    slot = list_slot[list_ids.reshape(-1)].astype(jnp.int32)
    totals = jax.ops.segment_sum(vec.astype(jnp.float32), slot, num_segments=LISTS)
    list_counts = jax.ops.segment_sum(jnp.ones(slot.shape, jnp.int32), slot, num_segments=LISTS).astype(jnp.int32)
    residual_sums = totals - list_counts.astype(jnp.float32)[:, None] * centroids
    return (layer_out, residual_sums, list_counts)
```

```python
import jax
import jax.numpy as jnp
from jax import lax
from jax.experimental import pallas as pl
from jax.experimental.pallas import tpu as pltpu
from jax.sharding import PartitionSpec as P

KV_HEADS = 4
HD = 128
Q_HEADS = 16


rope_base = 1000000.0
bf16 = jnp.bfloat16
f32 = jnp.float32


def rotate(values, places):
    half = HD // 2
    freq = rope_base ** (-(2.0 / HD) * jnp.arange(half, dtype=jnp.float32))
    angle = places.astype(jnp.float32)[:, None] * freq[None, :]
    cosine = jnp.cos(angle)[:, None, :]
    sine = jnp.sin(angle)[:, None, :]
    shaped = values.reshape(values.shape[0], -1, HD)
    first = shaped[..., :half]
    second = shaped[..., half:]
    turned = jnp.concatenate(
        [first * cosine - second * sine, second * cosine + first * sine], axis=-1
    )
    return turned.reshape(values.shape)


def positions_of(lengths_row, token_count, caption_count):
    ends = jnp.cumsum(lengths_row, dtype=jnp.int32)
    index = jnp.arange(token_count, dtype=jnp.int32)
    segment = jnp.sum((index[:, None] >= ends[None, :]).astype(jnp.int32), axis=1, dtype=jnp.int32)
    member = segment[None, :] == jnp.arange(caption_count, dtype=jnp.int32)[:, None]
    starts = ends - lengths_row
    place = index - jnp.sum(jnp.where(member, starts[:, None], 0), axis=0, dtype=jnp.int32)
    return (segment, member, place)


def wide_slice_shards(
    hidden,
    lengths,
    list_ids,
    list_slot,
    gain,
    w_query,
    b_query,
    w_keyval,
    b_keyval,
    w_out,
    w_pool,
    centroids,
):
    token_count = hidden.shape[0]
    caption_count = lengths.shape[1]
    dp_count = lax.axis_size("dp")
    tp_index = lax.axis_index("tp")
    wide = hidden.astype(jnp.float32)
    normed = (wide * lax.rsqrt(jnp.mean(wide * wide, axis=1, keepdims=True) + 1e-06) * gain).astype(
        jnp.bfloat16
    )
    segment, member, place = positions_of(lengths[0], token_count, caption_count)
    query_cols = w_query.shape[1]
    kv_width = b_keyval.shape[0] // 2
    head_group = tp_index * (query_cols // HD) // (Q_HEADS // KV_HEADS)
    full_cols = lax.all_gather(w_keyval, "tp", axis=1, tiled=True)
    query_sum = jnp.dot(
        normed,
        lax.all_gather(w_query, "dp", axis=0, tiled=True),
        preferred_element_type=jnp.float32,
    )
    own_cols = jnp.concatenate(
        [
            lax.dynamic_slice_in_dim(full_cols, head_group * HD, HD, 1),
            lax.dynamic_slice_in_dim(full_cols, kv_width + head_group * HD, HD, 1),
        ],
        axis=1,
    )
    keyval_sum = jnp.dot(
        normed,
        lax.all_gather(own_cols, "dp", axis=0, tiled=True),
        preferred_element_type=jnp.float32,
    )
    key_bias = lax.dynamic_slice_in_dim(b_keyval, head_group * HD, HD, 0)
    value_bias = lax.dynamic_slice_in_dim(b_keyval, kv_width + head_group * HD, HD, 0)
    keys = rotate(keyval_sum[:, :HD] + key_bias.astype(jnp.float32), place).astype(jnp.bfloat16)
    values = (keyval_sum[:, HD:] + value_bias.astype(jnp.float32)).astype(jnp.bfloat16)
    query = rotate(query_sum + b_query.astype(jnp.float32), place).astype(jnp.bfloat16)
    grouped = query.reshape(token_count, query_cols // HD, HD)
    scores = jnp.einsum("sgd,td->gst", grouped, keys, preferred_element_type=jnp.float32) * HD ** (
        -0.5
    )
    allowed = segment[:, None] == segment[None, :]
    scores = jnp.where(allowed[None], scores, -1e30)
    probs = jax.nn.softmax(scores, axis=-1).astype(jnp.bfloat16)
    attn = jnp.einsum("gst,td->sgd", probs, values, preferred_element_type=jnp.float32)
    attn = attn.astype(jnp.bfloat16).reshape(token_count, query_cols)
    partial_out = jnp.dot(
        attn, lax.all_gather(w_out, "dp", axis=1, tiled=True), preferred_element_type=jnp.float32
    )
    summed = lax.psum_scatter(
        partial_out.astype(jnp.bfloat16), "tp", scatter_dimension=1, tiled=True
    ).astype(jnp.float32)
    feature_share = summed.shape[1]
    own_input = lax.dynamic_slice_in_dim(wide, tp_index * feature_share, feature_share, 1)
    layer_out = (own_input + summed).astype(jnp.bfloat16)
    pooled = jnp.dot(member.astype(jnp.bfloat16), layer_out, preferred_element_type=jnp.float32)
    pooled = (pooled / lengths[0].astype(jnp.float32)[:, None]).astype(jnp.bfloat16)
    pooled_part = jnp.dot(pooled, w_pool, preferred_element_type=jnp.float32)
    vec = lax.psum_scatter(pooled_part.astype(jnp.bfloat16), "tp", scatter_dimension=1, tiled=True)
    lists_total = list_slot.shape[0]
    caption_lists = list_ids.reshape(-1)
    slot = jnp.sum(
        jnp.where(
            caption_lists[:, None] == jnp.arange(lists_total, dtype=jnp.int32)[None, :],
            list_slot[None, :],
            0,
        ),
        axis=1,
        dtype=jnp.int32,
    )
    lists_own = centroids.shape[0]
    send_cap = max(2, 2 * caption_count // dp_count)
    owner = slot // lists_own
    local = slot % lists_own
    order = jnp.arange(caption_count, dtype=jnp.int32)
    earlier = (owner[None, :] == owner[:, None]) & (order[None, :] < order[:, None])
    rank = jnp.sum(earlier.astype(jnp.int32), axis=1, dtype=jnp.int32)
    target = owner * send_cap + rank
    placed = jnp.arange(dp_count * send_cap, dtype=jnp.int32)[:, None] == target[None, :]
    send_values = jnp.dot(
        placed.astype(jnp.bfloat16), vec, preferred_element_type=jnp.float32
    ).astype(jnp.bfloat16)
    send_values = send_values.reshape(dp_count, send_cap, vec.shape[1])
    send_rows = jnp.sum(jnp.where(placed, local[None, :] + 1, 0), axis=1, dtype=jnp.int32).reshape(
        dp_count, send_cap
    )
    got_values, got_rows = (
        lax.all_to_all(send_values, "dp", split_axis=0, concat_axis=0, tiled=True),
        lax.all_to_all(send_rows, "dp", split_axis=0, concat_axis=0, tiled=True),
    )
    got_values = got_values.reshape(dp_count * send_cap, vec.shape[1])
    got_rows = got_rows.reshape(dp_count * send_cap)
    hits = got_rows[None, :] - 1 == jnp.arange(lists_own, dtype=jnp.int32)[:, None]
    totals = jnp.dot(hits.astype(jnp.bfloat16), got_values, preferred_element_type=jnp.float32)
    list_counts = jnp.sum(hits.astype(jnp.int32), axis=1, dtype=jnp.int32)
    residual_sums = totals - list_counts.astype(jnp.float32)[:, None] * centroids
    return (layer_out, residual_sums, list_counts)


def attention_kernel(q_own, q_oth, key_ref, value_ref, cos_ref, sin_ref, seg_col, seg_row, out_ref):
    def turn(x, cosine, sine):
        return (x * cosine + pltpu.roll(x, HD // 2, 1) * sine).astype(bf16)

    keys = turn(key_ref[...], cos_ref[...], sin_ref[...])
    values = value_ref[...].astype(bf16)
    rows = 128
    tokens = key_ref.shape[0]
    for i in range(tokens // rows):
        at = pl.ds(i * rows, rows)
        cosine, sine = cos_ref[at, :], sin_ref[at, :]
        allowed = seg_col[at, :] == seg_row[...]
        for part, ref in enumerate((q_own, q_oth)):
            heads = ref.shape[1] // HD
            for h in range(heads):
                query = turn(ref[at, h * HD : (h + 1) * HD], cosine, sine)
                scores = lax.dot_general(
                    query, keys, (((1,), (1,)), ((), ())), preferred_element_type=f32
                ) * HD ** (-0.5)
                scores = jnp.where(allowed, scores, -1e30)
                top = jnp.max(scores, axis=1, keepdims=True)
                weights = jnp.exp(scores - top)
                probs = (weights / jnp.sum(weights, axis=1, keepdims=True)).astype(bf16)
                mixed = jnp.dot(probs, values, preferred_element_type=f32)
                lo = (part * heads + h) * HD
                out_ref[at, lo : lo + HD] = mixed.astype(bf16)


def attend(q_own, q_oth, keys, values, cosine, sine, segment):
    tokens = q_own.shape[0]
    return pl.pallas_call(
        attention_kernel,
        out_shape=jax.ShapeDtypeStruct((tokens, q_own.shape[1] * 2), bf16),
        compiler_params=pltpu.CompilerParams(vmem_limit_bytes=32 * 1024 * 1024),
        cost_estimate=pl.CostEstimate(
            flops=4 * tokens * tokens * q_own.shape[1] * 2,
            bytes_accessed=8 * 1024 * 1024,
            transcendentals=tokens * tokens * 4,
        ),
    )(q_own, q_oth, keys, values, cosine, sine, segment[:, None], segment[None, :])


def folded_ring(n):
    return list(range(0, 1)) + list(range(1, n, 2)) + list(range(2 * ((n - 1) // 2), 0, -2))


def shards(
    hidden,
    lengths,
    list_ids,
    list_slot,
    gain,
    w_query,
    b_query,
    w_keyval,
    b_keyval,
    w_out,
    w_pool,
    centroids,
):
    tokens, width = hidden.shape
    captions = lengths.shape[1]
    n_dp, n_tp = lax.axis_size("dp"), lax.axis_size("tp")
    g, z, t = lax.axis_index("groups"), lax.axis_index("dp"), lax.axis_index("tp")
    ring = folded_ring(n_dp)
    place_in = {v: i for i, v in enumerate(ring)}
    ring_pairs = [(ring[i], ring[(i + 1) % n_dp]) for i in range(n_dp)]
    source_of = [[ring[(place_in[d] - m) % n_dp] for m in range(n_dp)] for d in range(n_dp)]
    blocks_at = jnp.array(source_of, jnp.int32)[z]
    blk = [blocks_at[m] for m in range(n_dp)]
    swap = [(0, 1), (1, 0)]
    core = [(i, i ^ 1) for i in range(n_tp)]
    share = width // n_dp

    q_half = w_query.shape[1] // 2
    o_half = w_out.shape[0] // 2

    def half(w, i, size, axis):
        return lax.dynamic_slice_in_dim(w, i * size, size, axis)

    q0 = (half(w_query, g, q_half, 1), half(w_query, 1 - g, q_half, 1))
    per_dev = w_keyval.shape[1] // HD
    rounds = [[] for _ in range(per_dev)]
    for gg in range(2):
        for tt in range(n_tp):
            head = tt * (w_query.shape[1] // HD) // (Q_HEADS // KV_HEADS)
            col = gg * KV_HEADS + head
            rounds[col % per_dev].append((gg * n_tp + col // per_dev, gg * n_tp + tt))
    came = [
        lax.ppermute(w_keyval[:, r * HD : (r + 1) * HD], ("groups", "tp"), rounds[r])
        for r in range(per_dev)
    ]
    head = t * (w_query.shape[1] // HD) // (Q_HEADS // KV_HEADS)
    kv_own = came[0]
    for r in range(1, per_dev):
        kv_own = jnp.where(head % per_dev == r, came[r], kv_own)
    cut = 512
    oa0 = half(w_out[:, :cut], g, o_half, 0)
    ob0 = half(w_out[:, cut:], g, o_half, 0)

    order = []
    for m in range(1, n_dp):
        order += [("q", m), ("k", m)]
    for m in range(1, n_dp):
        order += [("a", m), ("b", m)]
    zres = {("q", 0): q0[0], ("k", 0): kv_own, ("a", 0): oa0, ("b", 0): ob0}
    yres = {("q", 0): q0[1]}
    for i, key in enumerate(order):
        operand = zres[(key[0], key[1] - 1)]
        ties = []
        if i >= 2:
            ties.append((zres, order[i - 2]))
        if i >= 4:
            ties.append((yres, order[i - 4]))
        if ties:
            got = lax.optimization_barrier((operand, *[d[k] for d, k in ties]))
            operand = got[0]
            for (d, k), v in zip(ties, got[1:]):
                d[k] = v
        zres[key] = lax.ppermute(operand, "dp", ring_pairs)
        yres[key] = lax.ppermute(zres[key], "groups", swap)
        if i == 1:
            yres[("k", 0)] = lax.ppermute(kv_own, "groups", swap)

    wide = hidden.astype(f32)
    normed = (wide * lax.rsqrt(jnp.mean(wide * wide, axis=1, keepdims=True) + 1e-06) * gain).astype(
        bf16
    )
    segment, member, place = positions_of(lengths[0], tokens, captions)
    freq = rope_base ** (-(2.0 / HD) * jnp.arange(HD // 2, dtype=f32))
    angle = place.astype(f32)[:, None] * freq[None, :]
    cosine, sine = jnp.cos(angle), jnp.sin(angle)
    cosine = jnp.concatenate([cosine, cosine], axis=1)
    sine = jnp.concatenate([-sine, sine], axis=1)

    sums = {}
    for m in range(n_dp):
        rows = lax.dynamic_slice_in_dim(normed, blk[m] * share, share, 1)
        for name, res in (("q", zres), ("k", zres), ("Q", yres), ("K", yres)):
            part = jnp.dot(rows, res[(name.lower(), m)], preferred_element_type=f32)
            sums[name] = sums[name] + part if name in sums else part
    bq = b_query.astype(f32)
    q_own = sums["q"] + half(bq, g, q_half, 0)
    q_oth = sums["Q"] + half(bq, 1 - g, q_half, 0)
    kv_width = b_keyval.shape[0] // 2
    bkv = b_keyval.astype(f32)
    keys = jnp.where(g == 0, sums["k"], sums["K"]) + half(bkv, head, HD, 0)
    values = jnp.where(g == 0, sums["K"], sums["k"]) + lax.dynamic_slice_in_dim(
        bkv, kv_width + head * HD, HD, 0
    )
    attn = attend(q_own, q_oth, keys, values, cosine, sine, segment)

    inverse = 1.0 / lengths[0].astype(f32)[:, None]
    member16 = member.astype(bf16)
    pooled_hidden = jnp.dot(member16, hidden, preferred_element_type=f32) * inverse
    lists_total = list_slot.shape[0]
    slot = jnp.sum(
        jnp.where(
            list_ids.reshape(-1)[:, None] == jnp.arange(lists_total, dtype=jnp.int32)[None, :],
            list_slot[None, :],
            0,
        ),
        axis=1,
        dtype=jnp.int32,
    )
    early = jnp.concatenate(
        [
            pooled_hidden.astype(bf16).reshape(captions, n_dp, share).transpose(1, 0, 2),
            jnp.broadcast_to(slot.astype(bf16)[None, :, None], (n_dp, captions, HD)),
        ],
        axis=2,
    )
    early = lax.all_to_all(early, "dp", split_axis=0, concat_axis=0, tiled=True)
    slots = early[:, :, share].astype(jnp.int32)
    hits = slots[:, None, :] == jnp.arange(lists_total, dtype=jnp.int32)[None, :, None]
    hits16 = hits.astype(bf16)
    counts = jnp.sum(hits.astype(jnp.int32), axis=(0, 2), dtype=jnp.int32)
    lists_own = centroids.shape[0]
    list_counts = lax.dynamic_slice_in_dim(counts, z * lists_own, lists_own, 0)
    hidden_lists = jnp.einsum(
        "dlc,dcf->lf", hits16, early[:, :, :share], preferred_element_type=f32
    )
    pooled_attn = (jnp.dot(member16, attn, preferred_element_type=f32) * inverse).astype(bf16)
    attn_lists = jnp.zeros((lists_total, attn.shape[1]), f32)
    for m in range(n_dp):
        pairs = [(source_of[d][m], d) for d in range(n_dp)]
        came_pool = lax.ppermute(pooled_attn, "dp", pairs) if m else pooled_attn
        hit = lax.dynamic_index_in_dim(hits16, blk[m], 0, keepdims=False)
        attn_lists = attn_lists + jnp.dot(hit, came_pool, preferred_element_type=f32)
    attn_lists = attn_lists.astype(bf16)
    own_rows, oth_rows = half(w_out, g, o_half, 0), half(w_out, 1 - g, o_half, 0)
    pooled_lists = (
        jnp.dot(attn_lists[:, :o_half], own_rows, preferred_element_type=f32)
        + jnp.dot(attn_lists[:, o_half:], oth_rows, preferred_element_type=f32)
        + hidden_lists * (1.0 / n_tp)
    ).astype(bf16)
    across = lax.ppermute(
        w_pool, ("dp", "tp"), [(d * n_tp + d, d * n_tp + (d ^ 2)) for d in range(n_dp)]
    )
    have = jnp.where(t == z, w_pool, across)
    beside = lax.ppermute(
        have,
        ("dp", "tp"),
        [(d * n_tp + (d ^ k), d * n_tp + (d ^ k ^ 1)) for d in range(n_dp) for k in (0, 2)],
    )
    holds = (t == z) | (t == (z ^ 2))
    vec_lists = jnp.dot(
        jnp.where(holds, pooled_lists, 0), have, preferred_element_type=f32
    ) + jnp.dot(pooled_lists, beside, preferred_element_type=f32)
    cols = centroids.shape[1]
    late = vec_lists.astype(bf16).reshape(n_dp, lists_own, n_tp, cols).transpose(0, 2, 1, 3)
    late = late.reshape(n_dp * n_tp, lists_own, cols)
    late = lax.all_to_all(late, ("dp", "tp"), split_axis=0, concat_axis=0, tiled=True)
    totals = jnp.sum(late.astype(f32), axis=0)
    residual_sums = totals - list_counts.astype(f32)[:, None] * centroids

    c = t % 2
    rows_half = tokens // 2
    own_cols = slice(0, o_half)
    oth_cols = slice(o_half, 2 * o_half)

    def project(own, oth):
        out = jnp.dot(attn[:, own_cols], own, preferred_element_type=f32)
        out = out + jnp.dot(attn[:, oth_cols], oth, preferred_element_type=f32)
        return out.astype(bf16)

    def reduce_block(part, m):
        keep = half(part, c, rows_half, 0)
        sent = lax.ppermute(half(part, 1 - c, rows_half, 0), "tp", core)
        pair = (keep.astype(f32) + sent.astype(f32)).astype(bf16)
        pairs = []
        for d in range(n_dp):
            j = source_of[d][m]
            for k in (2, 3):
                pairs.append((d * n_tp + (j ^ k), d * n_tp + (j ^ k ^ 2)))
        came = lax.ppermute(pair, ("dp", "tp"), pairs)
        return pair.astype(f32) + came.astype(f32)

    sums_a, sums_b = [], []
    for m in range(n_dp):
        if m == 0:
            pa = project(oa0, half(w_out[:, :cut], 1 - g, o_half, 0))
            pb = project(ob0, half(w_out[:, cut:], 1 - g, o_half, 0))
        else:
            pa = project(zres[("a", m)], yres[("a", m)])
            pb = project(zres[("b", m)], yres[("b", m)])
        if m < n_dp - 1:
            whole = reduce_block(jnp.concatenate([pa, pb], axis=1), m)
            sums_a.append(whole[:, :cut])
            sums_b.append(whole[:, cut:])
        else:
            sums_a.append(reduce_block(pa, m))
            sums_b.append(reduce_block(pb, m))

    def chosen(index):
        a, b = sums_a[0], sums_b[0]
        for m in range(1, n_dp):
            a = jnp.where(blk[m] == index, sums_a[m], a)
            b = jnp.where(blk[m] == index, sums_b[m], b)
        return jnp.concatenate([a, b], axis=1)

    mine = chosen(t)
    other = lax.ppermute(chosen(t ^ 1).astype(bf16), "tp", core).astype(f32)
    first = jnp.where(c == 0, mine, other)
    second = jnp.where(c == 0, other, mine)
    summed = jnp.concatenate([first, second], axis=0)
    own_input = lax.dynamic_slice_in_dim(hidden, t * share, share, 1).astype(f32)
    layer_out = (own_input + summed).astype(bf16)
    return (layer_out, residual_sums, list_counts)


def solution(mesh):
    sizes = mesh.shape
    square = sizes["groups"] == 2 and sizes["dp"] == 4 and sizes["tp"] == 4
    return jax.shard_map(
        shards if square else wide_slice_shards,
        mesh=mesh,
        in_specs=(
            P(("groups", "dp"), None),
            P(("groups", "dp"), None),
            P(("groups", "dp"), None),
            P("groups"),
            P(),
            P("dp", "tp"),
            P("tp"),
            P("dp", "tp"),
            P(),
            P("tp", "dp"),
            P("tp", None),
            P("dp", "tp"),
        ),
        out_specs=(P(("groups", "dp"), "tp"), P(("groups", "dp"), "tp"), P(("groups", "dp"))),
        check_vma=False,
    )
```

```python
import jax
import jax.numpy as jnp
from jax import lax
from jax.experimental import pallas as pl
from jax.experimental.pallas import tpu as pltpu
from jax.sharding import PartitionSpec as P

KV_HEADS = 4
HD = 128
Q_HEADS = 16


rope_base = 1000000.0
bf16 = jnp.bfloat16
f32 = jnp.float32


def rotate(values, places):
    half = HD // 2
    freq = rope_base ** (-(2.0 / HD) * jnp.arange(half, dtype=jnp.float32))
    angle = places.astype(jnp.float32)[:, None] * freq[None, :]
    cosine = jnp.cos(angle)[:, None, :]
    sine = jnp.sin(angle)[:, None, :]
    shaped = values.reshape(values.shape[0], -1, HD)
    first = shaped[..., :half]
    second = shaped[..., half:]
    turned = jnp.concatenate(
        [first * cosine - second * sine, second * cosine + first * sine], axis=-1
    )
    return turned.reshape(values.shape)


def positions_of(lengths_row, token_count, caption_count):
    ends = jnp.cumsum(lengths_row, dtype=jnp.int32)
    index = jnp.arange(token_count, dtype=jnp.int32)
    segment = jnp.sum((index[:, None] >= ends[None, :]).astype(jnp.int32), axis=1, dtype=jnp.int32)
    member = segment[None, :] == jnp.arange(caption_count, dtype=jnp.int32)[:, None]
    starts = ends - lengths_row
    place = index - jnp.sum(jnp.where(member, starts[:, None], 0), axis=0, dtype=jnp.int32)
    return (segment, member, place)


def wide_slice_shards(
    hidden,
    lengths,
    list_ids,
    list_slot,
    gain,
    w_query,
    b_query,
    w_keyval,
    b_keyval,
    w_out,
    w_pool,
    centroids,
):
    token_count = hidden.shape[0]
    caption_count = lengths.shape[1]
    dp_count = lax.axis_size("dp")
    tp_index = lax.axis_index("tp")
    wide = hidden.astype(jnp.float32)
    normed = (wide * lax.rsqrt(jnp.mean(wide * wide, axis=1, keepdims=True) + 1e-06) * gain).astype(
        jnp.bfloat16
    )
    segment, member, place = positions_of(lengths[0], token_count, caption_count)
    query_cols = w_query.shape[1]
    kv_width = b_keyval.shape[0] // 2
    head_group = tp_index * (query_cols // HD) // (Q_HEADS // KV_HEADS)
    full_cols = lax.all_gather(w_keyval, "tp", axis=1, tiled=True)
    query_sum = jnp.dot(
        normed,
        lax.all_gather(w_query, "dp", axis=0, tiled=True),
        preferred_element_type=jnp.float32,
    )
    own_cols = jnp.concatenate(
        [
            lax.dynamic_slice_in_dim(full_cols, head_group * HD, HD, 1),
            lax.dynamic_slice_in_dim(full_cols, kv_width + head_group * HD, HD, 1),
        ],
        axis=1,
    )
    keyval_sum = jnp.dot(
        normed,
        lax.all_gather(own_cols, "dp", axis=0, tiled=True),
        preferred_element_type=jnp.float32,
    )
    key_bias = lax.dynamic_slice_in_dim(b_keyval, head_group * HD, HD, 0)
    value_bias = lax.dynamic_slice_in_dim(b_keyval, kv_width + head_group * HD, HD, 0)
    keys = rotate(keyval_sum[:, :HD] + key_bias.astype(jnp.float32), place).astype(jnp.bfloat16)
    values = (keyval_sum[:, HD:] + value_bias.astype(jnp.float32)).astype(jnp.bfloat16)
    query = rotate(query_sum + b_query.astype(jnp.float32), place).astype(jnp.bfloat16)
    grouped = query.reshape(token_count, query_cols // HD, HD)
    scores = jnp.einsum("sgd,td->gst", grouped, keys, preferred_element_type=jnp.float32) * HD ** (
        -0.5
    )
    allowed = segment[:, None] == segment[None, :]
    scores = jnp.where(allowed[None], scores, -1e30)
    probs = jax.nn.softmax(scores, axis=-1).astype(jnp.bfloat16)
    attn = jnp.einsum("gst,td->sgd", probs, values, preferred_element_type=jnp.float32)
    attn = attn.astype(jnp.bfloat16).reshape(token_count, query_cols)
    partial_out = jnp.dot(
        attn, lax.all_gather(w_out, "dp", axis=1, tiled=True), preferred_element_type=jnp.float32
    )
    summed = lax.psum_scatter(
        partial_out.astype(jnp.bfloat16), "tp", scatter_dimension=1, tiled=True
    ).astype(jnp.float32)
    feature_share = summed.shape[1]
    own_input = lax.dynamic_slice_in_dim(wide, tp_index * feature_share, feature_share, 1)
    layer_out = (own_input + summed).astype(jnp.bfloat16)
    pooled = jnp.dot(member.astype(jnp.bfloat16), layer_out, preferred_element_type=jnp.float32)
    pooled = (pooled / lengths[0].astype(jnp.float32)[:, None]).astype(jnp.bfloat16)
    pooled_part = jnp.dot(pooled, w_pool, preferred_element_type=jnp.float32)
    vec = lax.psum_scatter(pooled_part.astype(jnp.bfloat16), "tp", scatter_dimension=1, tiled=True)
    lists_total = list_slot.shape[0]
    caption_lists = list_ids.reshape(-1)
    slot = jnp.sum(
        jnp.where(
            caption_lists[:, None] == jnp.arange(lists_total, dtype=jnp.int32)[None, :],
            list_slot[None, :],
            0,
        ),
        axis=1,
        dtype=jnp.int32,
    )
    lists_own = centroids.shape[0]
    send_cap = max(2, 2 * caption_count // dp_count)
    owner = slot // lists_own
    local = slot % lists_own
    order = jnp.arange(caption_count, dtype=jnp.int32)
    earlier = (owner[None, :] == owner[:, None]) & (order[None, :] < order[:, None])
    rank = jnp.sum(earlier.astype(jnp.int32), axis=1, dtype=jnp.int32)
    target = owner * send_cap + rank
    placed = jnp.arange(dp_count * send_cap, dtype=jnp.int32)[:, None] == target[None, :]
    send_values = jnp.dot(
        placed.astype(jnp.bfloat16), vec, preferred_element_type=jnp.float32
    ).astype(jnp.bfloat16)
    send_values = send_values.reshape(dp_count, send_cap, vec.shape[1])
    send_rows = jnp.sum(jnp.where(placed, local[None, :] + 1, 0), axis=1, dtype=jnp.int32).reshape(
        dp_count, send_cap
    )
    got_values, got_rows = (
        lax.all_to_all(send_values, "dp", split_axis=0, concat_axis=0, tiled=True),
        lax.all_to_all(send_rows, "dp", split_axis=0, concat_axis=0, tiled=True),
    )
    got_values = got_values.reshape(dp_count * send_cap, vec.shape[1])
    got_rows = got_rows.reshape(dp_count * send_cap)
    hits = got_rows[None, :] - 1 == jnp.arange(lists_own, dtype=jnp.int32)[:, None]
    totals = jnp.dot(hits.astype(jnp.bfloat16), got_values, preferred_element_type=jnp.float32)
    list_counts = jnp.sum(hits.astype(jnp.int32), axis=1, dtype=jnp.int32)
    residual_sums = totals - list_counts.astype(jnp.float32)[:, None] * centroids
    return (layer_out, residual_sums, list_counts)


def prep_kernel(sc, hidden_ref, gain_ref, member_ref, blocks_ref, own_ref, pooled_ref):
    wide = hidden_ref[...].astype(f32)
    scale = lax.rsqrt(jnp.mean(wide * wide, axis=1, keepdims=True) + 1e-06)
    n, _, share = blocks_ref.shape
    for m in range(n):
        at = pl.ds(pl.multiple_of(sc[m] * share, 128), share)
        part = hidden_ref[:, at].astype(f32)
        blocks_ref[m] = (part * scale * gain_ref[:, at]).astype(bf16)
    own = hidden_ref[:, pl.ds(pl.multiple_of(sc[4] * share, 128), share)]
    own_ref[...] = own
    total = jnp.dot(member_ref[...], own, preferred_element_type=f32)

    @pl.when(pl.program_id(0) == 0)
    def _():
        pooled_ref[...] = jnp.zeros_like(pooled_ref)

    pooled_ref[...] += total


def prepare(scalars, hidden, gain, member, n):
    tokens, width = hidden.shape
    share = width // n
    captions = member.shape[0]
    rows = 128
    return pl.pallas_call(
        prep_kernel,
        grid_spec=pltpu.PrefetchScalarGridSpec(
            num_scalar_prefetch=1,
            grid=(tokens // rows,),
            in_specs=[
                pl.BlockSpec((rows, width), lambda i, s: (i, 0)),
                pl.BlockSpec((1, width), lambda i, s: (0, 0)),
                pl.BlockSpec((captions, rows), lambda i, s: (0, i)),
            ],
            out_specs=[
                pl.BlockSpec((n, rows, share), lambda i, s: (0, i, 0)),
                pl.BlockSpec((rows, share), lambda i, s: (i, 0)),
                pl.BlockSpec((captions, share), lambda i, s: (0, 0)),
            ],
        ),
        out_shape=[
            jax.ShapeDtypeStruct((n, tokens, share), bf16),
            jax.ShapeDtypeStruct((tokens, share), bf16),
            jax.ShapeDtypeStruct((captions, share), f32),
        ],
        compiler_params=pltpu.CompilerParams(vmem_limit_bytes=32 * 1024 * 1024),
        cost_estimate=pl.CostEstimate(
            flops=8 * tokens * width, bytes_accessed=4 * tokens * width, transcendentals=0
        ),
    )(scalars, hidden, gain[None, :], member)


def attention_kernel(
    sc,
    own_ref,
    oth_ref,
    bq_ref,
    bkv_ref,
    cos_ref,
    sin_ref,
    seg_col,
    seg_row,
    member_ref,
    inverse_ref,
    hits_ref,
    out_ref,
    lists_ref,
):
    def turn(x, cosine, sine):
        return (x * cosine + pltpu.roll(x, HD // 2, 1) * sine).astype(bf16)

    t, c, g = sc[4], sc[5], sc[6]
    tokens = own_ref.shape[0]
    wide = own_ref.shape[1] - HD
    heads = wide // HD
    kv_width = bkv_ref.shape[1] // 2
    at_key = pl.ds(pl.multiple_of(t * HD, HD), HD)
    at_value = pl.ds(pl.multiple_of(kv_width + t * HD, HD), HD)
    first, second = own_ref[:, wide:], oth_ref[:, wide:]
    keys = jnp.where(g == 0, first, second) + bkv_ref[:, at_key]
    values = (jnp.where(g == 0, second, first) + bkv_ref[:, at_value]).astype(bf16)
    keys = turn(keys, cos_ref[...], sin_ref[...])
    rows = 128
    per_half = tokens // 2 // rows
    pooled = jnp.zeros((member_ref.shape[0], 2 * wide), f32)
    for i in range(tokens // rows):
        at = pl.ds(i * rows, rows)
        cosine, sine = cos_ref[at, :], sin_ref[at, :]
        allowed = seg_col[at, :] == seg_row[...]
        slot = jnp.bitwise_xor(c, i // per_half)
        to = pl.ds((i % per_half) * rows, rows)
        out = []
        for part, ref in enumerate((own_ref, oth_ref)):
            for h in range(heads):
                lo = h * HD
                bias_at = pl.ds(
                    pl.multiple_of(jnp.bitwise_xor(g, part) * wide + lo, HD), HD
                )
                query = turn(ref[at, lo : lo + HD] + bq_ref[:, bias_at], cosine, sine)
                scores = lax.dot_general(
                    query, keys, (((1,), (1,)), ((), ())), preferred_element_type=f32
                ) * HD ** (-0.5)
                scores = jnp.where(allowed, scores, -1e30)
                top = jnp.max(scores, axis=1, keepdims=True)
                weights = jnp.exp(scores - top)
                probs = (weights / jnp.sum(weights, axis=1, keepdims=True)).astype(bf16)
                out.append(jnp.dot(probs, values, preferred_element_type=f32).astype(bf16))
        out = jnp.concatenate(out, axis=1)
        out_ref[slot, to, :] = out
        pooled = pooled + jnp.dot(member_ref[:, at], out, preferred_element_type=f32)
    pooled = (pooled * inverse_ref[...]).astype(bf16)
    lists_ref[...] = jnp.dot(hits_ref[...], pooled, preferred_element_type=f32).astype(bf16)


def attend(scalars, own, oth, bq, bkv, cosine, sine, segment, member, inverse, hits):
    tokens = own.shape[0]
    query_cols = 2 * (own.shape[1] - HD)
    vmem = pl.BlockSpec(memory_space=pltpu.VMEM)
    return pl.pallas_call(
        attention_kernel,
        in_specs=[pl.BlockSpec(memory_space=pltpu.SMEM)] + [vmem] * 11,
        out_specs=[vmem] * 2,
        out_shape=[
            jax.ShapeDtypeStruct((2, tokens // 2, query_cols), bf16),
            jax.ShapeDtypeStruct((hits.shape[0], query_cols), bf16),
        ],
        compiler_params=pltpu.CompilerParams(vmem_limit_bytes=32 * 1024 * 1024),
        cost_estimate=pl.CostEstimate(
            flops=4 * tokens * tokens * query_cols,
            bytes_accessed=8 * 1024 * 1024,
            transcendentals=tokens * tokens * query_cols // HD,
        ),
    )(
        scalars,
        own,
        oth,
        bq[None, :],
        bkv[None, :],
        cosine,
        sine,
        segment[:, None],
        segment[None, :],
        member,
        inverse,
        hits,
    )


def folded_ring(n):
    return [0] + list(range(1, n, 2)) + list(range(2 * ((n - 1) // 2), 0, -2))


def after(value, *earlier):
    return lax.optimization_barrier((value, *earlier))[0]


def shards(
    hidden,
    lengths,
    list_ids,
    list_slot,
    gain,
    w_query,
    b_query,
    w_keyval,
    b_keyval,
    w_out,
    w_pool,
    centroids,
):
    tokens, width = hidden.shape
    captions = lengths.shape[1]
    n_dp, n_tp = lax.axis_size("dp"), lax.axis_size("tp")
    share = width // n_dp
    ring = folded_ring(n_dp)
    place_in = {v: i for i, v in enumerate(ring)}
    source_of = [[ring[(place_in[d] - m) % n_dp] for m in range(n_dp)] for d in range(n_dp)]
    forward = [(ring[i], ring[(i + 1) % n_dp]) for i in range(n_dp)]
    backward = [(b, a) for a, b in forward]
    swap = [(0, 1), (1, 0)]
    core = [(i, i ^ 1) for i in range(n_tp)]
    across = [(i, i ^ 2) for i in range(n_tp)]
    table = []
    for gg in range(2):
        for d in range(n_dp):
            for tt in range(n_tp):
                chip = [source_of[d][m] // 2 == tt // 2 for m in range(n_dp)]
                mine = tt in (source_of[d][0], source_of[d][2])
                table.append(
                    [*source_of[d], tt, tt % 2, gg, int(chip[0]), int(chip[1]), int(mine), int(tt == d), d]
                )
    scalars = lax.dynamic_slice_in_dim(
        jnp.array(table, jnp.int32), lax.axis_index(("groups", "dp", "tp")), 1, 0
    )[0]
    g, t, z = lax.axis_index("groups"), lax.axis_index("tp"), lax.axis_index("dp")
    first_group = g == 0
    here_0, here_1, mine_a = scalars[7] == 1, scalars[8] == 1, scalars[9] == 1

    q_half = w_query.shape[1] // 2
    o_half = w_out.shape[0] // 2
    per_dev = w_keyval.shape[1] // HD
    rounds = [[] for _ in range(per_dev)]
    for gg in range(2):
        for tt in range(n_tp):
            col = gg * KV_HEADS + tt
            rounds[col % per_dev].append((gg * n_tp + col // per_dev, gg * n_tp + tt))
    came = [
        lax.ppermute(w_keyval[:, r * HD : (r + 1) * HD], ("groups", "tp"), rounds[r])
        for r in range(per_dev)
    ]
    kv_own = came[0]
    for r in range(1, per_dev):
        kv_own = jnp.where(t % per_dev == r, came[r], kv_own)
    o_own = jnp.where(first_group, w_out[:o_half], w_out[o_half:])
    o_oth = jnp.where(first_group, w_out[o_half:], w_out[:o_half])
    q_own = jnp.where(first_group, w_query[:, :q_half], w_query[:, q_half:])
    q_oth = jnp.where(first_group, w_query[:, q_half:], w_query[:, :q_half])
    qk_own = jnp.concatenate([q_own, kv_own], axis=1)
    cut = share // 256 * 128

    o_f = lax.ppermute(o_own, "dp", forward)
    qk_f = lax.ppermute(qk_own, "dp", forward)
    qk_r = lax.ppermute(qk_own, "dp", backward)
    kv_y = lax.ppermute(kv_own, "groups", swap)
    o_fy = lax.ppermute(o_f, "groups", swap)
    qk_fy = lax.ppermute(qk_f, "groups", swap)
    qk_s = lax.ppermute(after(qk_f, o_fy), "dp", forward)
    qk_ry = lax.ppermute(qk_r, "groups", swap)
    o_r = lax.ppermute(after(o_own, qk_r), "dp", backward)
    qk_sy = lax.ppermute(qk_s, "groups", swap)
    o_sa = lax.ppermute(after(o_f[:, :cut], qk_s), "dp", forward)
    o_ry = lax.ppermute(o_r, "groups", swap)
    o_sb = lax.ppermute(after(o_f[:, cut:], o_r), "dp", forward)
    o_say = lax.ppermute(o_sa, "groups", swap)
    o_sby = lax.ppermute(o_sb, "groups", swap)

    segment, member, place = positions_of(lengths[0], tokens, captions)
    member = member.astype(bf16)
    freq = rope_base ** (-(2.0 / HD) * jnp.arange(HD // 2, dtype=f32))
    angle = place.astype(f32)[:, None] * freq[None, :]
    cosine, sine = jnp.cos(angle), jnp.sin(angle)
    cosine = jnp.concatenate([cosine, cosine], axis=1)
    sine = jnp.concatenate([-sine, sine], axis=1)
    blocks, own_input, pooled_hidden = prepare(scalars, hidden, gain, member, n_dp)
    inverse = 1.0 / lengths[0].astype(f32)[:, None]
    pooled_hidden = (pooled_hidden * inverse).astype(bf16)
    lists_total = list_slot.shape[0]
    slot = jnp.sum(
        jnp.where(
            list_ids.reshape(-1)[:, None] == jnp.arange(lists_total, dtype=jnp.int32)[None, :],
            list_slot[None, :],
            0,
        ),
        axis=1,
        dtype=jnp.int32,
    )
    hits = (jnp.arange(lists_total, dtype=jnp.int32)[:, None] == slot[None, :]).astype(bf16)
    local_counts = jnp.sum(hits.astype(f32), axis=1)
    hidden_lists = jnp.dot(hits, pooled_hidden, preferred_element_type=f32)

    def dot(a, b):
        return jnp.dot(a, b, preferred_element_type=f32)

    qk_oth = jnp.concatenate([q_oth, kv_y], axis=1)
    sum_own = dot(blocks[0], qk_own) + dot(blocks[1], qk_f)
    sum_own = sum_own + dot(blocks[3], qk_r) + dot(blocks[2], qk_s)
    sum_oth = dot(blocks[0], qk_oth) + dot(blocks[1], qk_fy)
    sum_oth = sum_oth + dot(blocks[3], qk_ry) + dot(blocks[2], qk_sy)
    attn, attn_lists = attend(
        scalars,
        sum_own,
        sum_oth,
        b_query.astype(f32),
        b_keyval.astype(f32),
        cosine,
        sine,
        segment,
        member,
        inverse,
        hits,
    )

    lists_sum = attn_lists.astype(f32)
    for m in range(1, n_dp):
        pairs = [(source_of[d][m], d) for d in range(n_dp)]
        lists_sum = lists_sum + lax.ppermute(attn_lists, "dp", pairs).astype(f32)
    lists_sum = lists_sum.astype(bf16)
    plane = (dot(lists_sum[:, :q_half], o_own) + dot(lists_sum[:, q_half:], o_oth)).astype(bf16)
    plane = plane.astype(f32) + lax.ppermute(plane, "tp", core).astype(f32)
    plane16 = plane.astype(bf16)
    plane = plane + lax.ppermute(plane16, "tp", across).astype(f32)
    plane = (jnp.where(t == z, plane, 0.0) + hidden_lists).astype(bf16)
    vec_lists = dot(plane, w_pool).astype(bf16)
    lists_own, cols = centroids.shape
    late = vec_lists.reshape(n_dp, lists_own, n_tp, cols).transpose(0, 2, 1, 3)
    late = jnp.concatenate(
        [
            late,
            jnp.broadcast_to(
                local_counts.astype(bf16).reshape(n_dp, 1, lists_own, 1),
                (n_dp, n_tp, lists_own, HD),
            ),
        ],
        axis=3,
    ).reshape(n_dp * n_tp, lists_own, cols + HD)
    late = lax.all_to_all(late, ("dp", "tp"), split_axis=0, concat_axis=0, tiled=True)
    late = late.reshape(n_dp, n_tp, lists_own, cols + HD).astype(f32)
    totals = jnp.sum(late[..., :cols], axis=(0, 1))
    counts = jnp.sum(late[:, 0, :, cols], axis=0)
    residual_sums = totals - counts[:, None] * centroids
    list_counts = counts.astype(jnp.int32)

    def project(rows, own, oth):
        return (dot(rows[:, :q_half], own) + dot(rows[:, q_half:], oth)).astype(bf16)

    def reduce_pair(weights_a, weights_b, a_here):
        sent = jnp.concatenate([project(attn[1], *weights_a), project(attn[1], *weights_b)], axis=1)
        came = lax.ppermute(sent, "tp", core).astype(f32)
        n = weights_a[0].shape[1]
        sum_a = project(attn[0], *weights_a).astype(f32) + came[:, :n]
        sum_b = project(attn[0], *weights_b).astype(f32) + came[:, n:]
        stays = jnp.where(a_here, sum_a, sum_b)
        goes = jnp.where(a_here, sum_b, sum_a).astype(bf16)
        return stays + lax.ppermute(goes, "tp", across).astype(f32)

    block_b = reduce_pair((o_f, o_fy), (o_r, o_ry), here_1)
    block_aa = reduce_pair((o_own[:, :cut], o_oth[:, :cut]), (o_sa, o_say), here_0)
    block_ab = reduce_pair((o_own[:, cut:], o_oth[:, cut:]), (o_sb, o_sby), here_0)
    block_a = jnp.concatenate([block_aa, block_ab], axis=1)
    keep = jnp.where(mine_a, block_a, block_b)
    give = jnp.where(mine_a, block_b, block_a).astype(bf16)
    got = lax.ppermute(give, "tp", core).astype(f32)
    low = t % 2 == 0
    summed = jnp.concatenate([jnp.where(low, keep, got), jnp.where(low, got, keep)], axis=0)
    layer_out = (own_input.astype(f32) + summed).astype(bf16)
    return (layer_out, residual_sums, list_counts)


def solution(mesh):
    sizes = mesh.shape
    square = sizes["groups"] == 2 and sizes["dp"] == 4 and sizes["tp"] == 4
    return jax.shard_map(
        shards if square else wide_slice_shards,
        mesh=mesh,
        in_specs=(
            P(("groups", "dp"), None),
            P(("groups", "dp"), None),
            P(("groups", "dp"), None),
            P("groups"),
            P(),
            P("dp", "tp"),
            P("tp"),
            P("dp", "tp"),
            P(),
            P("tp", "dp"),
            P("tp", None),
            P("dp", "tp"),
        ),
        out_specs=(P(("groups", "dp"), "tp"), P(("groups", "dp"), "tp"), P(("groups", "dp"))),
        check_vma=False,
    )
```

```python
import functools

import jax
import jax.numpy as jnp
import numpy as np
from jax import lax
from jax.experimental import pallas as pl
from jax.experimental.pallas import tpu as pltpu
from jax.sharding import PartitionSpec as P

KV_HEADS = 4
HD = 128
Q_HEADS = 16


rope_base = 1000000.0
bf16 = jnp.bfloat16
f32 = jnp.float32


def rotate(values, places):
    half = HD // 2
    freq = rope_base ** (-(2.0 / HD) * jnp.arange(half, dtype=jnp.float32))
    angle = places.astype(jnp.float32)[:, None] * freq[None, :]
    cosine = jnp.cos(angle)[:, None, :]
    sine = jnp.sin(angle)[:, None, :]
    shaped = values.reshape(values.shape[0], -1, HD)
    first = shaped[..., :half]
    second = shaped[..., half:]
    turned = jnp.concatenate(
        [first * cosine - second * sine, second * cosine + first * sine], axis=-1
    )
    return turned.reshape(values.shape)


def positions_of(lengths_row, token_count, caption_count):
    ends = jnp.cumsum(lengths_row, dtype=jnp.int32)
    index = jnp.arange(token_count, dtype=jnp.int32)
    segment = jnp.sum((index[:, None] >= ends[None, :]).astype(jnp.int32), axis=1, dtype=jnp.int32)
    member = segment[None, :] == jnp.arange(caption_count, dtype=jnp.int32)[:, None]
    starts = ends - lengths_row
    place = index - jnp.sum(jnp.where(member, starts[:, None], 0), axis=0, dtype=jnp.int32)
    return (segment, member, place)


def wide_slice_shards(
    hidden,
    lengths,
    list_ids,
    list_slot,
    gain,
    w_query,
    b_query,
    w_keyval,
    b_keyval,
    w_out,
    w_pool,
    centroids,
):
    token_count = hidden.shape[0]
    caption_count = lengths.shape[1]
    dp_count = lax.axis_size("dp")
    tp_index = lax.axis_index("tp")
    wide = hidden.astype(jnp.float32)
    normed = (wide * lax.rsqrt(jnp.mean(wide * wide, axis=1, keepdims=True) + 1e-06) * gain).astype(
        jnp.bfloat16
    )
    segment, member, place = positions_of(lengths[0], token_count, caption_count)
    query_cols = w_query.shape[1]
    kv_width = b_keyval.shape[0] // 2
    head_group = tp_index * (query_cols // HD) // (Q_HEADS // KV_HEADS)
    full_cols = lax.all_gather(w_keyval, "tp", axis=1, tiled=True)
    query_sum = jnp.dot(
        normed,
        lax.all_gather(w_query, "dp", axis=0, tiled=True),
        preferred_element_type=jnp.float32,
    )
    own_cols = jnp.concatenate(
        [
            lax.dynamic_slice_in_dim(full_cols, head_group * HD, HD, 1),
            lax.dynamic_slice_in_dim(full_cols, kv_width + head_group * HD, HD, 1),
        ],
        axis=1,
    )
    keyval_sum = jnp.dot(
        normed,
        lax.all_gather(own_cols, "dp", axis=0, tiled=True),
        preferred_element_type=jnp.float32,
    )
    key_bias = lax.dynamic_slice_in_dim(b_keyval, head_group * HD, HD, 0)
    value_bias = lax.dynamic_slice_in_dim(b_keyval, kv_width + head_group * HD, HD, 0)
    keys = rotate(keyval_sum[:, :HD] + key_bias.astype(jnp.float32), place).astype(jnp.bfloat16)
    values = (keyval_sum[:, HD:] + value_bias.astype(jnp.float32)).astype(jnp.bfloat16)
    query = rotate(query_sum + b_query.astype(jnp.float32), place).astype(jnp.bfloat16)
    grouped = query.reshape(token_count, query_cols // HD, HD)
    scores = jnp.einsum("sgd,td->gst", grouped, keys, preferred_element_type=jnp.float32) * HD ** (
        -0.5
    )
    allowed = segment[:, None] == segment[None, :]
    scores = jnp.where(allowed[None], scores, -1e30)
    probs = jax.nn.softmax(scores, axis=-1).astype(jnp.bfloat16)
    attn = jnp.einsum("gst,td->sgd", probs, values, preferred_element_type=jnp.float32)
    attn = attn.astype(jnp.bfloat16).reshape(token_count, query_cols)
    partial_out = jnp.dot(
        attn, lax.all_gather(w_out, "dp", axis=1, tiled=True), preferred_element_type=jnp.float32
    )
    summed = lax.psum_scatter(
        partial_out.astype(jnp.bfloat16), "tp", scatter_dimension=1, tiled=True
    ).astype(jnp.float32)
    feature_share = summed.shape[1]
    own_input = lax.dynamic_slice_in_dim(wide, tp_index * feature_share, feature_share, 1)
    layer_out = (own_input + summed).astype(jnp.bfloat16)
    pooled = jnp.dot(member.astype(jnp.bfloat16), layer_out, preferred_element_type=jnp.float32)
    pooled = (pooled / lengths[0].astype(jnp.float32)[:, None]).astype(jnp.bfloat16)
    pooled_part = jnp.dot(pooled, w_pool, preferred_element_type=jnp.float32)
    vec = lax.psum_scatter(pooled_part.astype(jnp.bfloat16), "tp", scatter_dimension=1, tiled=True)
    lists_total = list_slot.shape[0]
    caption_lists = list_ids.reshape(-1)
    slot = jnp.sum(
        jnp.where(
            caption_lists[:, None] == jnp.arange(lists_total, dtype=jnp.int32)[None, :],
            list_slot[None, :],
            0,
        ),
        axis=1,
        dtype=jnp.int32,
    )
    lists_own = centroids.shape[0]
    send_cap = max(2, 2 * caption_count // dp_count)
    owner = slot // lists_own
    local = slot % lists_own
    order = jnp.arange(caption_count, dtype=jnp.int32)
    earlier = (owner[None, :] == owner[:, None]) & (order[None, :] < order[:, None])
    rank = jnp.sum(earlier.astype(jnp.int32), axis=1, dtype=jnp.int32)
    target = owner * send_cap + rank
    placed = jnp.arange(dp_count * send_cap, dtype=jnp.int32)[:, None] == target[None, :]
    send_values = jnp.dot(
        placed.astype(jnp.bfloat16), vec, preferred_element_type=jnp.float32
    ).astype(jnp.bfloat16)
    send_values = send_values.reshape(dp_count, send_cap, vec.shape[1])
    send_rows = jnp.sum(jnp.where(placed, local[None, :] + 1, 0), axis=1, dtype=jnp.int32).reshape(
        dp_count, send_cap
    )
    got_values, got_rows = (
        lax.all_to_all(send_values, "dp", split_axis=0, concat_axis=0, tiled=True),
        lax.all_to_all(send_rows, "dp", split_axis=0, concat_axis=0, tiled=True),
    )
    got_values = got_values.reshape(dp_count * send_cap, vec.shape[1])
    got_rows = got_rows.reshape(dp_count * send_cap)
    hits = got_rows[None, :] - 1 == jnp.arange(lists_own, dtype=jnp.int32)[:, None]
    totals = jnp.dot(hits.astype(jnp.bfloat16), got_values, preferred_element_type=jnp.float32)
    list_counts = jnp.sum(hits.astype(jnp.int32), axis=1, dtype=jnp.int32)
    residual_sums = totals - list_counts.astype(jnp.float32)[:, None] * centroids
    return (layer_out, residual_sums, list_counts)


VMEM = pl.BlockSpec(memory_space=pltpu.VMEM)
SMEM = pl.BlockSpec(memory_space=pltpu.SMEM)
T, GROUP, KEEP_0, KEEP_1, MINE_A, KEY_FROM, VALUE_FROM = range(4, 11)


def dot(a, b):
    return jnp.dot(a, b, preferred_element_type=f32)


def turn(x, cosine, sine):
    return x * cosine + pltpu.roll(x, HD // 2, 1) * sine


def lanes(start, size):
    return pl.ds(pl.multiple_of(start, 128), size)


def call(kernel, outs, flops, scalars, *args):
    moved = sum(a.size * a.dtype.itemsize for a in (*args, *outs))
    return pl.pallas_call(
        kernel,
        in_specs=[SMEM] + [VMEM] * len(args),
        out_specs=[VMEM] * len(outs),
        out_shape=outs,
        compiler_params=pltpu.CompilerParams(vmem_limit_bytes=60 * 1024 * 1024),
        cost_estimate=pl.CostEstimate(flops=flops, bytes_accessed=moved, transcendentals=0),
    )(scalars, *args)


def places_kernel(
    freq, lengths, ids, slots, cos_ref, sin_ref, seg_col, seg_row, member_ref, inverse_ref, hits_ref, counts_ref
):
    i32 = jnp.int32
    tokens = cos_ref.shape[0]
    captions = lengths.shape[1]
    lists = slots.shape[1]
    row = lengths[...]
    square = (captions, captions)
    down = lax.broadcasted_iota(i32, square, 0)
    along = lax.broadcasted_iota(i32, square, 1)
    wide_row = jnp.broadcast_to(row, square)
    col = jnp.sum(jnp.where(down == along, wide_row, 0), axis=1, keepdims=True)
    end_col = jnp.sum(jnp.where(along <= down, wide_row, 0), axis=1, keepdims=True)
    start_col = end_col - col
    end_row = jnp.sum(jnp.where(down <= along, jnp.broadcast_to(col, square), 0), axis=0, keepdims=True)
    start_row = end_row - row
    inverse_ref[...] = 1.0 / col.astype(f32)
    index = lax.broadcasted_iota(i32, (captions, tokens), 1)
    member_ref[...] = jnp.where((index >= start_col) & (index < end_col), 1.0, 0.0).astype(bf16)
    seg_row[...] = jnp.sum(jnp.where(index >= end_col, 1, 0), axis=0, keepdims=True)
    index = lax.broadcasted_iota(i32, (tokens, captions), 0)
    seg_col[...] = jnp.sum(jnp.where(index >= end_row, 1, 0), axis=1, keepdims=True)
    inside = (index >= start_row) & (index < end_row)
    place = jnp.sum(jnp.where(inside, index - start_row, 0), axis=1, keepdims=True)
    angle = place.astype(f32) * freq[...]
    cos_ref[...] = jnp.cos(angle)
    sine = jnp.sin(angle)
    lane = lax.broadcasted_iota(i32, (tokens, HD), 1)
    sin_ref[...] = jnp.where(lane < HD // 2, -sine, sine)
    square = (lists, lists)
    down = lax.broadcasted_iota(i32, square, 0)
    along = lax.broadcasted_iota(i32, square, 1)
    slot_col = jnp.sum(
        jnp.where(down == along, jnp.broadcast_to(slots[...], square), 0), axis=1, keepdims=True
    )
    down = lax.broadcasted_iota(i32, (lists, captions), 0)
    slot_row = jnp.sum(jnp.where(ids[...] == down, slot_col, 0), axis=0, keepdims=True)
    hits = jnp.where(down == slot_row, 1.0, 0.0)
    hits_ref[...] = hits.astype(bf16)
    counts_ref[...] = jnp.sum(hits, axis=1, keepdims=True)


def places(lengths, list_ids, list_slot, tokens):
    captions, lists = lengths.shape[1], list_slot.shape[0]
    freq = rope_base ** (-(2.0 / HD) * (np.arange(HD) % (HD // 2)))
    shape = jax.ShapeDtypeStruct
    return pl.pallas_call(
        places_kernel,
        in_specs=[VMEM] * 4,
        out_specs=[VMEM] * 8,
        out_shape=[
            shape((tokens, HD), f32),
            shape((tokens, HD), f32),
            shape((tokens, 1), jnp.int32),
            shape((1, tokens), jnp.int32),
            shape((captions, tokens), bf16),
            shape((captions, 1), f32),
            shape((lists, captions), bf16),
            shape((lists, 1), f32),
        ],
        compiler_params=pltpu.CompilerParams(vmem_limit_bytes=60 * 1024 * 1024),
        cost_estimate=pl.CostEstimate(
            flops=64 * tokens * HD, bytes_accessed=tokens * HD * 8, transcendentals=2 * tokens * HD
        ),
    )(jnp.asarray(freq, f32)[None, :], lengths, list_ids, list_slot[None, :])


def prep_kernel(sc, hidden_ref, gain_ref, member_ref, *outs):
    *block_refs, own_ref, pooled_ref = outs
    wide = hidden_ref[...].astype(f32)
    scale = lax.rsqrt(jnp.mean(wide * wide, axis=1, keepdims=True) + 1e-06)
    share = own_ref.shape[1]
    for m, ref in enumerate(block_refs):
        at = lanes(sc[m] * share, share)
        ref[...] = (hidden_ref[:, at].astype(f32) * scale * gain_ref[:, at]).astype(bf16)
    own = hidden_ref[:, lanes(sc[T] * share, share)]
    own_ref[...] = own

    @pl.when(pl.program_id(0) == 0)
    def _():
        pooled_ref[...] = jnp.zeros_like(pooled_ref)

    pooled_ref[...] += dot(member_ref[...], own)


def prepare(scalars, hidden, gain, member, n):
    tokens, width = hidden.shape
    share = width // n
    captions = member.shape[0]
    rows = 128
    stripe = pl.BlockSpec((rows, share), lambda i, s: (i, 0))
    return pl.pallas_call(
        prep_kernel,
        grid_spec=pltpu.PrefetchScalarGridSpec(
            num_scalar_prefetch=1,
            grid=(tokens // rows,),
            in_specs=[
                pl.BlockSpec((rows, width), lambda i, s: (i, 0)),
                pl.BlockSpec((1, width), lambda i, s: (0, 0)),
                pl.BlockSpec((captions, rows), lambda i, s: (0, i)),
            ],
            out_specs=[stripe] * (n + 1) + [pl.BlockSpec((captions, share), lambda i, s: (0, 0))],
        ),
        out_shape=[jax.ShapeDtypeStruct((tokens, share), bf16)] * (n + 1)
        + [jax.ShapeDtypeStruct((captions, share), f32)],
        compiler_params=pltpu.CompilerParams(vmem_limit_bytes=60 * 1024 * 1024),
        cost_estimate=pl.CostEstimate(
            flops=8 * tokens * width, bytes_accessed=4 * tokens * width, transcendentals=0
        ),
    )(scalars, hidden, gain[None, :], member)


def keyval_kernel(sc, b0, b1, b2, b3, w, r1, r2, r3, y1, y2, y3, bias, cos_ref, sin_ref, out_ref):
    g, t = sc[GROUP], sc[T]
    base = dot(b0[...], w[...])
    own = dot(b1[...], r1[...]) + dot(b2[...], r2[...]) + dot(b3[...], r3[...])
    oth = dot(b1[...], y1[...]) + dot(b2[...], y2[...]) + dot(b3[...], y3[...])
    heads = w.shape[1] // HD
    keyed = t * heads < KV_HEADS
    for h in range(heads):
        at = slice(h * HD, (h + 1) * HD)
        x = base[:, at] + jnp.where(g == h, own, oth)
        x = x + bias[:, lanes((t * heads + h) * HD, HD)].astype(f32)
        out_ref[:, at] = jnp.where(keyed, turn(x, cos_ref[...], sin_ref[...]), x).astype(bf16)


def query_kernel(sc, b0, b1, b2, b3, w, r1, r2, r3, y1, y3, own_ref, oth_ref):
    g = sc[GROUP]
    half = own_ref.shape[1]
    own = dot(b0[...], w[:, lanes(g * half, half)]) + dot(b1[...], r1[...])
    own_ref[...] = own + dot(b2[...], r2[...]) + dot(b3[...], r3[...])
    oth = dot(b0[...], w[:, lanes((1 - g) * half, half)]) + dot(b1[...], y1[...])
    oth_ref[...] = oth + dot(b3[...], y3[...])


def attention_kernel(
    sc,
    own_ref,
    oth_ref,
    b2,
    y2,
    bq_ref,
    x0,
    x1,
    x2,
    cos_ref,
    sin_ref,
    seg_col,
    seg_row,
    member_ref,
    inverse_ref,
    hits_ref,
    out_ref,
    lists_ref,
    query_ref,
):
    t, g = sc[T], sc[GROUP]
    tokens, wide = own_ref.shape
    heads = wide // HD
    here = lanes((t % (x0.shape[1] // HD)) * HD, HD)

    def pick(origin):
        return jnp.where(
            origin == 0, x0[:, here], jnp.where(origin == 1, x1[:, here], x2[:, here])
        )

    keys, values = pick(sc[KEY_FROM]), pick(sc[VALUE_FROM])
    query_ref[...] = oth_ref[...] + dot(b2[...], y2[...])
    rows = 128
    pooled = jnp.zeros((member_ref.shape[0], 2 * wide), f32)
    for i in range(tokens // rows):
        at = pl.ds(i * rows, rows)
        lo_key, hi_key = max(0, (i - 1) * rows), min(tokens, (i + 2) * rows)
        cosine, sine = cos_ref[at, :], sin_ref[at, :]
        allowed = seg_col[at, :] == seg_row[:, lo_key:hi_key]
        out = []
        for part, ref in enumerate((own_ref, query_ref)):
            for h in range(heads):
                lo = h * HD
                bias = bq_ref[:, lanes(jnp.bitwise_xor(g, part) * wide + lo, HD)].astype(f32)
                query = turn(ref[at, lo : lo + HD] + bias, cosine, sine).astype(bf16)
                scores = lax.dot_general(
                    query,
                    keys[lo_key:hi_key],
                    (((1,), (1,)), ((), ())),
                    preferred_element_type=f32,
                ) * HD ** (-0.5)
                scores = jnp.where(allowed, scores, -1e30)
                top = jnp.max(scores, axis=1, keepdims=True)
                weights = jnp.exp(scores - top)
                probs = (weights / jnp.sum(weights, axis=1, keepdims=True)).astype(bf16)
                out.append(dot(probs, values[lo_key:hi_key]).astype(bf16))
        out = jnp.concatenate(out, axis=1)
        out_ref[at, :] = out
        pooled = pooled + dot(member_ref[:, at], out)
    pooled = (pooled * inverse_ref[...]).astype(bf16)
    lists_ref[...] = dot(hits_ref[...], pooled).astype(bf16)


def attend(scalars, own, *rest):
    tokens, wide = own.shape
    lists = rest[-1].shape[0]
    outs = [
        jax.ShapeDtypeStruct((tokens, 2 * wide), bf16),
        jax.ShapeDtypeStruct((lists, 2 * wide), bf16),
    ]
    return pl.pallas_call(
        attention_kernel,
        in_specs=[SMEM] + [VMEM] * (1 + len(rest)),
        out_specs=[VMEM] * 2,
        out_shape=outs,
        scratch_shapes=[pltpu.VMEM((tokens, wide), f32)],
        compiler_params=pltpu.CompilerParams(vmem_limit_bytes=60 * 1024 * 1024),
        cost_estimate=pl.CostEstimate(
            flops=8 * tokens * tokens * wide,
            bytes_accessed=8 * 1024 * 1024,
            transcendentals=tokens * tokens * 2 * wide // HD,
        ),
    )(scalars, own, *rest)


def project(attn, weights, ref):
    half = attn.shape[1] // 2
    first, second = weights()
    ref[...] = (dot(attn[:, :half], first) + dot(attn[:, half:], second)).astype(bf16)


def project_two(keep, attn, first, second, sent, kept):
    @pl.when(keep == 1)
    def _():
        project(attn, first, kept)
        project(attn, second, sent)

    @pl.when(keep == 0)
    def _():
        project(attn, second, kept)
        project(attn, first, sent)


def project_own_kernel(sc, attn, w, own_b, oth_b, sent, kept):
    half = attn.shape[1] // 2
    g = sc[GROUP]

    def stored():
        return (
            w[pl.ds(pl.multiple_of(g * half, half), half), :],
            w[pl.ds(pl.multiple_of((1 - g) * half, half), half), :],
        )

    project_two(sc[KEEP_0], attn, stored, lambda: (own_b[...], oth_b[...]), sent, kept)


def project_kernel(lo, hi, sc, attn, own_a, oth_a, own_b, oth_b, sent, kept):
    project_two(
        sc[KEEP_1],
        attn,
        lambda: (own_a[:, lo:hi], oth_a[:, lo:hi]),
        lambda: (own_b[...], oth_b[...]),
        sent,
        kept,
    )


def add_kernel(sc, kept, came, total):
    total[...] = (kept[...].astype(f32) + came[...].astype(f32)).astype(bf16)


def finish_kernel(sc, own, ta, ca, tb0, cb0, tb1, cb1, out):
    cut = tb0.shape[1]
    mine = sc[MINE_A] == 1
    for lo, hi, t, c in ((0, cut, tb0, cb0), (cut, own.shape[1], tb1, cb1)):
        a = ta[:, lo:hi].astype(f32) + ca[:, lo:hi].astype(f32)
        b = t[...].astype(f32) + c[...].astype(f32)
        out[:, lo:hi] = (own[:, lo:hi].astype(f32) + jnp.where(mine, a, b)).astype(bf16)


def folded_ring(n):
    return [0] + list(range(1, n, 2)) + list(range(2 * ((n - 1) // 2), 0, -2))


def after(value, *earlier):
    return lax.optimization_barrier((value, *earlier))[0]


def shards(
    hidden,
    lengths,
    list_ids,
    list_slot,
    gain,
    w_query,
    b_query,
    w_keyval,
    b_keyval,
    w_out,
    w_pool,
    centroids,
):
    tokens, width = hidden.shape
    captions = lengths.shape[1]
    n_dp, n_tp = lax.axis_size("dp"), lax.axis_size("tp")
    share = width // n_dp
    ring = folded_ring(n_dp)
    place_in = {v: i for i, v in enumerate(ring)}
    source_of = [[ring[(place_in[d] - m) % n_dp] for m in range(n_dp)] for d in range(n_dp)]
    forward = [(ring[i], ring[(i + 1) % n_dp]) for i in range(n_dp)]
    backward = [(b, a) for a, b in forward]
    swap = [(0, 1), (1, 0)]
    core = [(i, i ^ 1) for i in range(n_tp)]
    across = [(i, i ^ 2) for i in range(n_tp)]
    per_dev = w_keyval.shape[1] // HD
    rounds = [[], []]
    origin = []
    for tt in range(n_tp):
        for source in (tt // per_dev, (KV_HEADS + tt) // per_dev):
            if source == tt:
                origin.append(0)
                continue
            for k, pairs in enumerate(rounds):
                if all(a != source and b != tt for a, b in pairs):
                    pairs.append((source, tt))
                    origin.append(k + 1)
                    break
    table = []
    for gg in range(2):
        for d in range(n_dp):
            for tt in range(n_tp):
                stays = [int(source_of[d][m] % 2 == tt % 2) for m in range(2)]
                mine = int(tt in (source_of[d][0], source_of[d][2]))
                table.append(
                    [*source_of[d], tt, gg, *stays, mine, *origin[2 * tt : 2 * tt + 2]]
                )
    scalars = lax.dynamic_slice_in_dim(
        jnp.array(table, jnp.int32),
        lax.axis_index(("groups", "dp", "tp")),
        1,
        0,
        allow_negative_indices=False,
    )[0]
    g, t, z = lax.axis_index("groups"), lax.axis_index("tp"), lax.axis_index("dp")

    def own_half(w, axis):
        size = w.shape[axis] // 2
        return lax.dynamic_slice_in_dim(w, g * size, size, axis, allow_negative_indices=False)

    cosine, sine, seg_col, seg_row, member, inverse, hits, local_counts = places(
        lengths, list_ids, list_slot, tokens
    )

    kv_own = own_half(w_keyval, 1)
    q_own = own_half(w_query, 1)
    o_own = own_half(w_out, 0)
    cut = share // 256 * 128 + 128

    own = {"k": kv_own, "q": q_own, "o": o_own, "a": o_own[:, :cut], "b": o_own[:, cut:]}
    stages = [["k1", "k3"], ["q1", "k2"], ["q3"], ["q2"], ["o1"], ["o2"], ["a3", "b3"]]
    lag = 3
    ring_of, swapped = {}, {}

    def run_stage(i, *ties):
        ties = list(ties)
        if i >= 1:
            ties += [ring_of[key] for key in stages[i - 1]]
        if lag <= i < len(stages) - 1:
            ties += [swapped[key] for key in stages[i - lag]]
        for key in stages[i]:
            piece = ring_of[key[0] + "1"] if key[1] == "2" else own[key[0]]
            pairs = backward if key[1] == "3" else forward
            ring_of[key] = lax.ppermute(after(piece, *ties) if ties else piece, "dp", pairs)
        for key in stages[i]:
            swapped[key] = lax.ppermute(ring_of[key], "groups", swap)

    run_stage(0)
    run_stage(1, cosine)
    *blocks, own_input, pooled_hidden = prepare(
        scalars, after(hidden, swapped["k1"], swapped["k3"]), gain, member, n_dp
    )
    run_stage(2, blocks[0])
    run_stage(3)
    run_stage(4)
    hidden_lists = dot(hits, (pooled_hidden * inverse).astype(bf16))

    shape = jax.ShapeDtypeStruct
    work = 2 * tokens * width
    (kv_mine,) = call(
        keyval_kernel,
        [shape((tokens, w_keyval.shape[1]), bf16)],
        work * w_keyval.shape[1],
        scalars,
        *blocks,
        w_keyval,
        *[r["k%d" % m] for r in (ring_of, swapped) for m in range(1, n_dp)],
        b_keyval[None, :],
        cosine,
        sine,
    )
    kv_came = [lax.ppermute(kv_mine, "tp", pairs) for pairs in rounds]
    run_stage(5, *kv_came)
    q_half = w_query.shape[1] // 2
    sum_own, sum_oth = call(
        query_kernel,
        [shape((tokens, q_half), f32)] * 2,
        work * q_half * 2,
        scalars,
        *blocks,
        w_query,
        *[ring_of[key] for key in ("q1", "q2", "q3")],
        *[swapped[key] for key in ("q1", "q3")],
    )
    run_stage(6, sum_own)
    attn, attn_lists = attend(
        scalars,
        after(sum_own, ring_of["o1"]),
        sum_oth,
        blocks[2],
        swapped["q2"],
        b_query[None, :],
        kv_mine,
        *kv_came,
        cosine,
        sine,
        seg_col,
        seg_row,
        member,
        inverse,
        hits,
    )

    def project_pair(kernel, n, attn, *weights):
        sent, kept = call(
            kernel,
            [shape((tokens, n), bf16)] * 2,
            4 * tokens * q_half * 2 * n,
            scalars,
            attn,
            *weights,
        )
        return sent, kept, lax.ppermute(sent, "tp", core)

    def exchange(kept, came, m):
        (total,) = call(
            add_kernel, [shape(kept.shape, bf16)], kept.size, scalars, kept, came
        )
        pairs = []
        for d in range(n_dp):
            for block in (source_of[d][m], source_of[d][m + 2]):
                pairs.append((d * n_tp + (block ^ 2), d * n_tp + block))
        return total, lax.ppermute(total, ("dp", "tp"), pairs)

    def both(key):
        return ring_of[key], swapped[key]

    sent_a, kept_a, came_a = project_pair(
        project_own_kernel, share, attn, w_out, *both("o2")
    )
    block_a = exchange(kept_a, after(came_a, swapped["a3"]), 0)

    attn_lists = after(attn_lists, ring_of["b3"])
    lists_sum = attn_lists.astype(f32)
    for m in range(1, n_dp):
        pairs = [(source_of[d][m], d) for d in range(n_dp)]
        lists_sum = lists_sum + lax.ppermute(attn_lists, "dp", pairs).astype(f32)
    lists_sum = after(lists_sum.astype(bf16), sent_a)
    first = jnp.where(g == 0, lists_sum[:, :q_half], lists_sum[:, q_half:])
    second = jnp.where(g == 0, lists_sum[:, q_half:], lists_sum[:, :q_half])
    plane = dot(jnp.concatenate([first, second], axis=1), w_out).astype(bf16)
    plane = plane.astype(f32) + lax.ppermute(plane, "tp", core).astype(f32)
    plane16 = after(plane.astype(bf16), block_a[0])
    crossed = lax.ppermute(plane16, "tp", across)
    rows = after(attn, block_a[0], plane16)
    sent_b0, kept_b0, came_b0 = project_pair(
        functools.partial(project_kernel, 0, cut), cut, rows, *both("o1"), *both("a3")
    )
    plane = after(plane, sent_b0)
    plane = plane + crossed.astype(f32)
    plane = (jnp.where(t == z, plane, 0.0) + hidden_lists).astype(bf16)
    vec_lists = dot(plane, w_pool).astype(bf16)
    lists_own, cols = centroids.shape
    late = vec_lists.reshape(n_dp, lists_own, n_tp, cols).transpose(0, 2, 1, 3)
    late = jnp.concatenate(
        [
            late,
            jnp.broadcast_to(
                local_counts.astype(bf16).reshape(n_dp, 1, lists_own, 1),
                (n_dp, n_tp, lists_own, HD),
            ),
        ],
        axis=3,
    ).reshape(n_dp * n_tp, lists_own, cols + HD)
    late = lax.all_to_all(late, ("dp", "tp"), split_axis=0, concat_axis=0, tiled=True)
    late = late.reshape(n_dp, n_tp, lists_own, cols + HD).astype(f32)
    totals = jnp.sum(late[..., :cols], axis=(0, 1))
    counts = jnp.sum(late[:, 0, :, cols], axis=0)
    residual_sums = totals - counts[:, None] * centroids
    list_counts = counts.astype(jnp.int32)
    block_b0 = exchange(kept_b0, after(came_b0, swapped["b3"]), 1)
    rows = after(rows, block_b0[0], vec_lists)
    _, kept_b1, came_b1 = project_pair(
        functools.partial(project_kernel, cut, share),
        share - cut,
        rows,
        *both("o1"),
        *both("b3"),
    )
    block_b1 = exchange(kept_b1, came_b1, 1)
    (layer_out,) = call(
        finish_kernel,
        [shape((tokens, share), bf16)],
        tokens * share,
        scalars,
        own_input,
        *block_a,
        *block_b0,
        *block_b1,
    )
    return (layer_out, residual_sums, list_counts)


def solution(mesh):
    sizes = mesh.shape
    square = sizes["groups"] == 2 and sizes["dp"] == 4 and sizes["tp"] == 4
    return jax.shard_map(
        shards if square else wide_slice_shards,
        mesh=mesh,
        in_specs=(
            P(("groups", "dp"), None),
            P(("groups", "dp"), None),
            P(("groups", "dp"), None),
            P("groups"),
            P(),
            P("dp", "tp"),
            P("tp"),
            P("dp", "tp"),
            P(),
            P("tp", "dp"),
            P("tp", None),
            P("dp", "tp"),
        ),
        out_specs=(P(("groups", "dp"), "tp"), P(("groups", "dp"), "tp"), P(("groups", "dp"))),
        check_vma=False,
    )
```

```python
import functools

import jax
import jax.numpy as jnp
import numpy as np
from jax import lax
from jax.experimental import pallas as pl
from jax.experimental.pallas import tpu as pltpu
from jax.sharding import PartitionSpec as P

KV_HEADS = 4
HD = 128
Q_HEADS = 16


rope_base = 1000000.0
bf16 = jnp.bfloat16
f32 = jnp.float32


def rotate(values, places):
    half = HD // 2
    freq = rope_base ** (-(2.0 / HD) * jnp.arange(half, dtype=jnp.float32))
    angle = places.astype(jnp.float32)[:, None] * freq[None, :]
    cosine = jnp.cos(angle)[:, None, :]
    sine = jnp.sin(angle)[:, None, :]
    shaped = values.reshape(values.shape[0], -1, HD)
    first = shaped[..., :half]
    second = shaped[..., half:]
    turned = jnp.concatenate(
        [first * cosine - second * sine, second * cosine + first * sine], axis=-1
    )
    return turned.reshape(values.shape)


def positions_of(lengths_row, token_count, caption_count):
    ends = jnp.cumsum(lengths_row, dtype=jnp.int32)
    index = jnp.arange(token_count, dtype=jnp.int32)
    segment = jnp.sum((index[:, None] >= ends[None, :]).astype(jnp.int32), axis=1, dtype=jnp.int32)
    member = segment[None, :] == jnp.arange(caption_count, dtype=jnp.int32)[:, None]
    starts = ends - lengths_row
    place = index - jnp.sum(jnp.where(member, starts[:, None], 0), axis=0, dtype=jnp.int32)
    return (segment, member, place)


def wide_slice_shards(
    hidden,
    lengths,
    list_ids,
    list_slot,
    gain,
    w_query,
    b_query,
    w_keyval,
    b_keyval,
    w_out,
    w_pool,
    centroids,
):
    token_count = hidden.shape[0]
    caption_count = lengths.shape[1]
    dp_count = lax.axis_size("dp")
    tp_index = lax.axis_index("tp")
    wide = hidden.astype(jnp.float32)
    normed = (wide * lax.rsqrt(jnp.mean(wide * wide, axis=1, keepdims=True) + 1e-06) * gain).astype(
        jnp.bfloat16
    )
    segment, member, place = positions_of(lengths[0], token_count, caption_count)
    query_cols = w_query.shape[1]
    kv_width = b_keyval.shape[0] // 2
    head_group = tp_index * (query_cols // HD) // (Q_HEADS // KV_HEADS)
    full_cols = lax.all_gather(w_keyval, "tp", axis=1, tiled=True)
    query_sum = jnp.dot(
        normed,
        lax.all_gather(w_query, "dp", axis=0, tiled=True),
        preferred_element_type=jnp.float32,
    )
    own_cols = jnp.concatenate(
        [
            lax.dynamic_slice_in_dim(full_cols, head_group * HD, HD, 1),
            lax.dynamic_slice_in_dim(full_cols, kv_width + head_group * HD, HD, 1),
        ],
        axis=1,
    )
    keyval_sum = jnp.dot(
        normed,
        lax.all_gather(own_cols, "dp", axis=0, tiled=True),
        preferred_element_type=jnp.float32,
    )
    key_bias = lax.dynamic_slice_in_dim(b_keyval, head_group * HD, HD, 0)
    value_bias = lax.dynamic_slice_in_dim(b_keyval, kv_width + head_group * HD, HD, 0)
    keys = rotate(keyval_sum[:, :HD] + key_bias.astype(jnp.float32), place).astype(jnp.bfloat16)
    values = (keyval_sum[:, HD:] + value_bias.astype(jnp.float32)).astype(jnp.bfloat16)
    query = rotate(query_sum + b_query.astype(jnp.float32), place).astype(jnp.bfloat16)
    grouped = query.reshape(token_count, query_cols // HD, HD)
    scores = jnp.einsum("sgd,td->gst", grouped, keys, preferred_element_type=jnp.float32) * HD ** (
        -0.5
    )
    allowed = segment[:, None] == segment[None, :]
    scores = jnp.where(allowed[None], scores, -1e30)
    probs = jax.nn.softmax(scores, axis=-1).astype(jnp.bfloat16)
    attn = jnp.einsum("gst,td->sgd", probs, values, preferred_element_type=jnp.float32)
    attn = attn.astype(jnp.bfloat16).reshape(token_count, query_cols)
    partial_out = jnp.dot(
        attn, lax.all_gather(w_out, "dp", axis=1, tiled=True), preferred_element_type=jnp.float32
    )
    summed = lax.psum_scatter(
        partial_out.astype(jnp.bfloat16), "tp", scatter_dimension=1, tiled=True
    ).astype(jnp.float32)
    feature_share = summed.shape[1]
    own_input = lax.dynamic_slice_in_dim(wide, tp_index * feature_share, feature_share, 1)
    layer_out = (own_input + summed).astype(jnp.bfloat16)
    pooled = jnp.dot(member.astype(jnp.bfloat16), layer_out, preferred_element_type=jnp.float32)
    pooled = (pooled / lengths[0].astype(jnp.float32)[:, None]).astype(jnp.bfloat16)
    pooled_part = jnp.dot(pooled, w_pool, preferred_element_type=jnp.float32)
    vec = lax.psum_scatter(pooled_part.astype(jnp.bfloat16), "tp", scatter_dimension=1, tiled=True)
    lists_total = list_slot.shape[0]
    caption_lists = list_ids.reshape(-1)
    slot = jnp.sum(
        jnp.where(
            caption_lists[:, None] == jnp.arange(lists_total, dtype=jnp.int32)[None, :],
            list_slot[None, :],
            0,
        ),
        axis=1,
        dtype=jnp.int32,
    )
    lists_own = centroids.shape[0]
    send_cap = max(2, 2 * caption_count // dp_count)
    owner = slot // lists_own
    local = slot % lists_own
    order = jnp.arange(caption_count, dtype=jnp.int32)
    earlier = (owner[None, :] == owner[:, None]) & (order[None, :] < order[:, None])
    rank = jnp.sum(earlier.astype(jnp.int32), axis=1, dtype=jnp.int32)
    target = owner * send_cap + rank
    placed = jnp.arange(dp_count * send_cap, dtype=jnp.int32)[:, None] == target[None, :]
    send_values = jnp.dot(
        placed.astype(jnp.bfloat16), vec, preferred_element_type=jnp.float32
    ).astype(jnp.bfloat16)
    send_values = send_values.reshape(dp_count, send_cap, vec.shape[1])
    send_rows = jnp.sum(jnp.where(placed, local[None, :] + 1, 0), axis=1, dtype=jnp.int32).reshape(
        dp_count, send_cap
    )
    got_values, got_rows = (
        lax.all_to_all(send_values, "dp", split_axis=0, concat_axis=0, tiled=True),
        lax.all_to_all(send_rows, "dp", split_axis=0, concat_axis=0, tiled=True),
    )
    got_values = got_values.reshape(dp_count * send_cap, vec.shape[1])
    got_rows = got_rows.reshape(dp_count * send_cap)
    hits = got_rows[None, :] - 1 == jnp.arange(lists_own, dtype=jnp.int32)[:, None]
    totals = jnp.dot(hits.astype(jnp.bfloat16), got_values, preferred_element_type=jnp.float32)
    list_counts = jnp.sum(hits.astype(jnp.int32), axis=1, dtype=jnp.int32)
    residual_sums = totals - list_counts.astype(jnp.float32)[:, None] * centroids
    return (layer_out, residual_sums, list_counts)


VMEM = pl.BlockSpec(memory_space=pltpu.VMEM)
SMEM = pl.BlockSpec(memory_space=pltpu.SMEM)
T, GROUP, KEEP_0, KEEP_1, MINE_A, KEY_FROM, VALUE_FROM, SEND_1, SEND_2 = range(4, 13)
TAIL = 20


def dot(a, b):
    return jnp.dot(a, b, preferred_element_type=f32)


def turn(x, cosine, sine):
    return x * cosine + pltpu.roll(x, HD // 2, 1) * sine


def lanes(start, size):
    return pl.ds(pl.multiple_of(start, 128), size)


def call(kernel, outs, flops, scalars, *args, vmem=60):
    moved = sum(a.size * a.dtype.itemsize for a in (*args, *outs))
    return pl.pallas_call(
        kernel,
        in_specs=[SMEM] + [VMEM] * len(args),
        out_specs=[VMEM] * len(outs),
        out_shape=outs,
        compiler_params=pltpu.CompilerParams(vmem_limit_bytes=vmem * 1024 * 1024),
        cost_estimate=pl.CostEstimate(flops=flops, bytes_accessed=moved, transcendentals=0),
    )(scalars, *args)


def places_kernel(
    freq, lengths, ids, slots, cos_ref, sin_ref, seg_col, seg_row, member_ref, inverse_ref, hits_ref, counts_ref
):
    i32 = jnp.int32
    tokens = cos_ref.shape[0]
    captions = lengths.shape[1]
    lists = slots.shape[1]
    row = lengths[...]
    square = (captions, captions)
    down = lax.broadcasted_iota(i32, square, 0)
    along = lax.broadcasted_iota(i32, square, 1)
    wide_row = jnp.broadcast_to(row, square)
    col = jnp.sum(jnp.where(down == along, wide_row, 0), axis=1, keepdims=True)
    end_col = jnp.sum(jnp.where(along <= down, wide_row, 0), axis=1, keepdims=True)
    start_col = end_col - col
    end_row = jnp.sum(jnp.where(down <= along, jnp.broadcast_to(col, square), 0), axis=0, keepdims=True)
    start_row = end_row - row
    inverse_ref[...] = 1.0 / col.astype(f32)
    index = lax.broadcasted_iota(i32, (captions, tokens), 1)
    member_ref[...] = jnp.where((index >= start_col) & (index < end_col), 1.0, 0.0).astype(bf16)
    seg_row[...] = jnp.sum(jnp.where(index >= end_col, 1, 0), axis=0, keepdims=True)
    index = lax.broadcasted_iota(i32, (tokens, captions), 0)
    seg_col[...] = jnp.sum(jnp.where(index >= end_row, 1, 0), axis=1, keepdims=True)
    inside = (index >= start_row) & (index < end_row)
    place = jnp.sum(jnp.where(inside, index - start_row, 0), axis=1, keepdims=True)
    angle = place.astype(f32) * freq[...]
    cos_ref[...] = jnp.cos(angle)
    sine = jnp.sin(angle)
    lane = lax.broadcasted_iota(i32, (tokens, HD), 1)
    sin_ref[...] = jnp.where(lane < HD // 2, -sine, sine)
    square = (lists, lists)
    down = lax.broadcasted_iota(i32, square, 0)
    along = lax.broadcasted_iota(i32, square, 1)
    slot_col = jnp.sum(
        jnp.where(down == along, jnp.broadcast_to(slots[...], square), 0), axis=1, keepdims=True
    )
    down = lax.broadcasted_iota(i32, (lists, captions), 0)
    slot_row = jnp.sum(jnp.where(ids[...] == down, slot_col, 0), axis=0, keepdims=True)
    hits = jnp.where(down == slot_row, 1.0, 0.0)
    hits_ref[...] = hits.astype(bf16)
    counts_ref[...] = jnp.sum(hits, axis=1, keepdims=True)


def places(lengths, list_ids, list_slot, tokens):
    captions, lists = lengths.shape[1], list_slot.shape[0]
    freq = rope_base ** (-(2.0 / HD) * (np.arange(HD) % (HD // 2)))
    shape = jax.ShapeDtypeStruct
    return pl.pallas_call(
        places_kernel,
        in_specs=[VMEM] * 4,
        out_specs=[VMEM] * 8,
        out_shape=[
            shape((tokens, HD), f32),
            shape((tokens, HD), f32),
            shape((tokens, 1), jnp.int32),
            shape((1, tokens), jnp.int32),
            shape((captions, tokens), bf16),
            shape((captions, 1), f32),
            shape((lists, captions), bf16),
            shape((lists, 1), f32),
        ],
        compiler_params=pltpu.CompilerParams(vmem_limit_bytes=60 * 1024 * 1024),
        cost_estimate=pl.CostEstimate(
            flops=64 * tokens * HD, bytes_accessed=tokens * HD * 8, transcendentals=2 * tokens * HD
        ),
    )(jnp.asarray(freq, f32)[None, :], lengths, list_ids, list_slot[None, :])


def prep_kernel(sc, hidden_ref, gain_ref, member_ref, *outs):
    *block_refs, own_ref, pooled_ref = outs
    wide = hidden_ref[...].astype(f32)
    scale = lax.rsqrt(jnp.mean(wide * wide, axis=1, keepdims=True) + 1e-06)
    share = own_ref.shape[1]
    for m, ref in enumerate(block_refs):
        at = lanes(sc[m] * share, share)
        ref[...] = (hidden_ref[:, at].astype(f32) * scale * gain_ref[:, at]).astype(bf16)
    own = hidden_ref[:, lanes(sc[T] * share, share)]
    own_ref[...] = own

    @pl.when(pl.program_id(0) == 0)
    def _():
        pooled_ref[...] = jnp.zeros_like(pooled_ref)

    pooled_ref[...] += dot(member_ref[...], own)


def prepare(scalars, hidden, gain, member, n):
    tokens, width = hidden.shape
    share = width // n
    captions = member.shape[0]
    rows = 128
    stripe = pl.BlockSpec((rows, share), lambda i, s: (i, 0))
    return pl.pallas_call(
        prep_kernel,
        grid_spec=pltpu.PrefetchScalarGridSpec(
            num_scalar_prefetch=1,
            grid=(tokens // rows,),
            in_specs=[
                pl.BlockSpec((rows, width), lambda i, s: (i, 0)),
                pl.BlockSpec((1, width), lambda i, s: (0, 0)),
                pl.BlockSpec((captions, rows), lambda i, s: (0, i)),
            ],
            out_specs=[stripe] * (n + 1) + [pl.BlockSpec((captions, share), lambda i, s: (0, 0))],
        ),
        out_shape=[jax.ShapeDtypeStruct((tokens, share), bf16)] * (n + 1)
        + [jax.ShapeDtypeStruct((captions, share), f32)],
        compiler_params=pltpu.CompilerParams(vmem_limit_bytes=60 * 1024 * 1024),
        cost_estimate=pl.CostEstimate(
            flops=8 * tokens * width, bytes_accessed=4 * tokens * width, transcendentals=0
        ),
    )(scalars, hidden, gain[None, :], member)


def projection_kernel(sc, b0, b1, b2, b3, wk, wq, r1, r2, r3, y1, y3, kv_ref, own_ref, oth_ref):
    g = sc[GROUP]
    half = own_ref.shape[1]
    own = dot(b1[...], r1[...]) + dot(b2[...], r2[...]) + dot(b3[...], r3[...])
    oth = dot(b1[...], y1[...]) + dot(b3[...], y3[...])
    base = dot(b0[...], wk[...])
    for h in range(wk.shape[1] // HD):
        at = slice(h * HD, (h + 1) * HD)
        kv_ref[:, at] = base[:, at] + jnp.where(g == h, own[:, :HD], oth[:, :HD])
    own_ref[...] = own[:, HD:] + dot(b0[...], wq[:, lanes(g * half, half)])
    oth_ref[...] = oth[:, HD:] + dot(b0[...], wq[:, lanes((1 - g) * half, half)])


def keyval_kernel(sc, kv_ref, b2, y2, bias, cos_ref, sin_ref, out_ref, send_1, send_2):
    g, t = sc[GROUP], sc[T]
    last = dot(b2[...], y2[:, :HD])
    heads = kv_ref.shape[1] // HD
    keyed = t * heads < KV_HEADS
    for h in range(heads):
        at = slice(h * HD, (h + 1) * HD)
        x = kv_ref[:, at] + jnp.where(g == h, 0.0, last)
        x = x + bias[:, lanes((t * heads + h) * HD, HD)].astype(f32)
        out_ref[:, at] = jnp.where(keyed, turn(x, cos_ref[...], sin_ref[...]), x).astype(bf16)
    send_1[...] = out_ref[:, lanes(sc[SEND_1] * HD, HD)]
    send_2[...] = out_ref[:, lanes(sc[SEND_2] * HD, HD)]


def attention_kernel(
    sc,
    own_ref,
    oth_ref,
    b2,
    y2,
    bq_ref,
    x0,
    x1,
    x2,
    cos_ref,
    sin_ref,
    seg_col,
    seg_row,
    member_ref,
    inverse_ref,
    hits_ref,
    out_ref,
    lists_ref,
    query_ref,
):
    t, g = sc[T], sc[GROUP]
    tokens, wide = own_ref.shape
    heads = wide // HD
    here = lanes((t % (x0.shape[1] // HD)) * HD, HD)

    def pick(origin):
        return jnp.where(
            origin == 0, x0[:, here], jnp.where(origin == 1, x1[...], x2[...])
        )

    keys, values = pick(sc[KEY_FROM]), pick(sc[VALUE_FROM])
    query_ref[...] = oth_ref[...] + dot(b2[...], y2[:, HD:])
    rows = 128
    pooled = jnp.zeros((member_ref.shape[0], 2 * wide), f32)
    for i in range(tokens // rows):
        at = pl.ds(i * rows, rows)
        lo_key, hi_key = max(0, (i - 1) * rows), min(tokens, (i + 2) * rows)
        cosine, sine = cos_ref[at, :], sin_ref[at, :]
        allowed = seg_col[at, :] == seg_row[:, lo_key:hi_key]
        out = []
        for part, ref in enumerate((own_ref, query_ref)):
            for h in range(heads):
                lo = h * HD
                bias = bq_ref[:, lanes(jnp.bitwise_xor(g, part) * wide + lo, HD)].astype(f32)
                query = turn(ref[at, lo : lo + HD] + bias, cosine, sine).astype(bf16)
                scores = lax.dot_general(
                    query,
                    keys[lo_key:hi_key],
                    (((1,), (1,)), ((), ())),
                    preferred_element_type=f32,
                ) * HD ** (-0.5)
                scores = jnp.where(allowed, scores, -1e30)
                top = jnp.max(scores, axis=1, keepdims=True)
                weights = jnp.exp(scores - top)
                probs = (weights / jnp.sum(weights, axis=1, keepdims=True)).astype(bf16)
                out.append(dot(probs, values[lo_key:hi_key]).astype(bf16))
        out = jnp.concatenate(out, axis=1)
        out_ref[at, :] = out
        pooled = pooled + dot(member_ref[:, at], out)
    pooled = (pooled * inverse_ref[...]).astype(bf16)
    lists_ref[...] = dot(hits_ref[...], pooled).astype(bf16)


def attend(scalars, own, *rest):
    tokens, wide = own.shape
    lists = rest[-1].shape[0]
    outs = [
        jax.ShapeDtypeStruct((tokens, 2 * wide), bf16),
        jax.ShapeDtypeStruct((lists, 2 * wide), bf16),
    ]
    return pl.pallas_call(
        attention_kernel,
        in_specs=[SMEM] + [VMEM] * (1 + len(rest)),
        out_specs=[VMEM] * 2,
        out_shape=outs,
        scratch_shapes=[pltpu.VMEM((tokens, wide), f32)],
        compiler_params=pltpu.CompilerParams(vmem_limit_bytes=60 * 1024 * 1024),
        cost_estimate=pl.CostEstimate(
            flops=8 * tokens * tokens * wide,
            bytes_accessed=8 * 1024 * 1024,
            transcendentals=tokens * tokens * 2 * wide // HD,
        ),
    )(scalars, own, *rest)


def project(attn, weights, ref):
    half = attn.shape[1] // 2
    left, right = attn[:, :half], attn[:, half:]
    lo = 0
    for first, second in weights():
        hi = lo + first.shape[1]
        ref[:, lo:hi] = (dot(left, first) + dot(right, second)).astype(bf16)
        lo = hi


def project_two(keep, attn, first, second, sent, kept):
    @pl.when(keep == 1)
    def _():
        project(attn, first, kept)
        project(attn, second, sent)

    @pl.when(keep == 0)
    def _():
        project(attn, second, kept)
        project(attn, first, sent)


def project_own_kernel(sc, attn, w, own_b, oth_b, sent, kept):
    half = attn.shape[1] // 2
    g = sc[GROUP]

    def stored():
        return [
            (
                w[pl.ds(pl.multiple_of(g * half, half), half), :],
                w[pl.ds(pl.multiple_of((1 - g) * half, half), half), :],
            )
        ]

    project_two(sc[KEEP_0], attn, stored, lambda: [(own_b[...], oth_b[...])], sent, kept)


def project_kernel(sc, attn, own_a, oth_a, own_b, oth_b, own_c, oth_c, sent, kept):
    project_two(
        sc[KEEP_1],
        attn,
        lambda: [(own_a[...], oth_a[...])],
        lambda: [(own_b[...], oth_b[...]), (own_c[...], oth_c[...])],
        sent,
        kept,
    )


def add_kernel(sc, kept, came, total):
    total[...] = (kept[...].astype(f32) + came[...].astype(f32)).astype(bf16)


def finish_kernel(sc, own, ta, ca, tb, cb, out):
    @pl.when(sc[MINE_A] == 1)
    def _():
        out[...] = (own[...].astype(f32) + (ta[...].astype(f32) + ca[...].astype(f32))).astype(bf16)

    @pl.when(sc[MINE_A] == 0)
    def _():
        out[...] = (own[...].astype(f32) + (tb[...].astype(f32) + cb[...].astype(f32))).astype(bf16)


def folded_ring(n):
    return [0] + list(range(1, n, 2)) + list(range(2 * ((n - 1) // 2), 0, -2))


def after(value, *earlier):
    return lax.optimization_barrier((value, *earlier))[0]


def shards(
    hidden,
    lengths,
    list_ids,
    list_slot,
    gain,
    w_query,
    b_query,
    w_keyval,
    b_keyval,
    w_out,
    w_pool,
    centroids,
):
    tokens, width = hidden.shape
    captions = lengths.shape[1]
    n_dp, n_tp = lax.axis_size("dp"), lax.axis_size("tp")
    share = width // n_dp
    ring = folded_ring(n_dp)
    place_in = {v: i for i, v in enumerate(ring)}
    source_of = [[ring[(place_in[d] - m) % n_dp] for m in range(n_dp)] for d in range(n_dp)]
    forward = [(ring[i], ring[(i + 1) % n_dp]) for i in range(n_dp)]
    backward = [(b, a) for a, b in forward]
    swap = [(0, 1), (1, 0)]
    core = [(i, i ^ 1) for i in range(n_tp)]
    across = [(i, i ^ 2) for i in range(n_tp)]
    per_dev = w_keyval.shape[1] // HD
    rounds = [[], []]
    sends = [[0] * n_tp, [0] * n_tp]
    origin = []
    for tt in range(n_tp):
        for head in (tt, KV_HEADS + tt):
            source = head // per_dev
            if source == tt:
                origin.append(0)
                continue
            for k, pairs in enumerate(rounds):
                if all(a != source and b != tt for a, b in pairs):
                    pairs.append((source, tt))
                    sends[k][source] = head % per_dev
                    origin.append(k + 1)
                    break
    table = []
    for gg in range(2):
        for d in range(n_dp):
            for tt in range(n_tp):
                stays = [int(source_of[d][m] % 2 == tt % 2) for m in range(2)]
                mine = int(tt in (source_of[d][0], source_of[d][2]))
                table.append(
                    [*source_of[d], tt, gg, *stays, mine, *origin[2 * tt : 2 * tt + 2], sends[0][tt], sends[1][tt]]
                )
    scalars = lax.dynamic_slice_in_dim(
        jnp.array(table, jnp.int32),
        lax.axis_index(("groups", "dp", "tp")),
        1,
        0,
        allow_negative_indices=False,
    )[0]
    g, t, z = lax.axis_index("groups"), lax.axis_index("tp"), lax.axis_index("dp")

    def own_half(w, axis):
        size = w.shape[axis] // 2
        return lax.dynamic_slice_in_dim(w, g * size, size, axis, allow_negative_indices=False)

    cosine, sine, seg_col, seg_row, member, inverse, hits, local_counts = places(
        lengths, list_ids, list_slot, tokens
    )

    kq_own = jnp.concatenate([own_half(w_keyval, 1), own_half(w_query, 1)], axis=1)
    o_own = own_half(w_out, 0)
    cut = share // 256 * 128 + 128

    own = {"q": kq_own, "o": o_own, "a": o_own[:, :cut], "b": o_own[:, cut:]}
    stages = [["q1"], ["q3"], ["q2"], ["o1", "a3"], ["o2", "b3"]]
    lag = 2
    ring_of, swapped = {}, {}

    def run_stage(i, *ties, swap_ties=()):
        ties = list(ties)
        if i >= 1:
            ties += [ring_of[key] for key in stages[i - 1]]
        if i >= lag:
            ties += [swapped[key] for key in stages[i - lag]]
        for key in stages[i]:
            piece = ring_of[key[0] + "1"] if key[1] == "2" else own[key[0]]
            pairs = backward if key[1] == "3" else forward
            ring_of[key] = lax.ppermute(after(piece, *ties) if ties else piece, "dp", pairs)
        for key in stages[i]:
            came = ring_of[key]
            if swap_ties:
                came = after(came, *swap_ties, *[ring_of[k] for k in stages[i]])
            swapped[key] = lax.ppermute(came, "groups", swap)

    run_stage(0)
    *blocks, own_input, pooled_hidden = prepare(scalars, hidden, gain, member, n_dp)
    run_stage(1, blocks[0], cosine)
    run_stage(2)
    run_stage(3)
    hidden_lists = dot(hits, (pooled_hidden * inverse).astype(bf16))

    shape = jax.ShapeDtypeStruct
    work = 2 * tokens * width
    q_half = w_query.shape[1] // 2
    kv_sum, sum_own, sum_oth = call(
        projection_kernel,
        [shape((tokens, w_keyval.shape[1]), f32)] + [shape((tokens, q_half), f32)] * 2,
        work * (q_half * 2 + w_keyval.shape[1]),
        scalars,
        *blocks,
        w_keyval,
        w_query,
        *[ring_of[key] for key in ("q1", "q2", "q3")],
        *[swapped[key] for key in ("q1", "q3")],
    )
    kv_mine, *kv_sent = call(
        keyval_kernel,
        [shape(kv_sum.shape, bf16)] + [shape((tokens, HD), bf16)] * 2,
        tokens * share * HD,
        scalars,
        kv_sum,
        blocks[2],
        swapped["q2"],
        b_keyval[None, :],
        cosine,
        sine,
    )
    kv_came = [lax.ppermute(x, "tp", pairs) for x, pairs in zip(kv_sent, rounds)]
    run_stage(4, sum_own, swap_ties=[*kv_came, swapped["o1"]])
    attn, attn_lists = attend(
        scalars,
        sum_own,
        sum_oth,
        blocks[2],
        swapped["q2"],
        b_query[None, :],
        kv_mine,
        *kv_came,
        cosine,
        sine,
        seg_col,
        seg_row,
        member,
        inverse,
        hits,
    )

    def project_pair(kernel, n, attn, *weights):
        sent, kept = call(
            kernel,
            [shape((tokens, n), bf16)] * 2,
            4 * tokens * q_half * 2 * n,
            scalars,
            attn,
            *weights,
            vmem=TAIL,
        )
        return sent, kept, lax.ppermute(sent, "tp", core)

    def exchange(kept, came, m):
        (total,) = call(
            add_kernel, [shape(kept.shape, bf16)], kept.size, scalars, kept, came, vmem=TAIL
        )
        pairs = []
        for d in range(n_dp):
            for block in (source_of[d][m], source_of[d][m + 2]):
                pairs.append((d * n_tp + (block ^ 2), d * n_tp + block))
        return total, lax.ppermute(total, ("dp", "tp"), pairs)

    def both(key):
        return ring_of[key], swapped[key]

    sent_a, kept_a, came_a = project_pair(project_own_kernel, share, attn, w_out, *both("o2"))
    block_a = exchange(kept_a, came_a, 0)

    attn_lists = after(attn_lists, ring_of["o2"], ring_of["b3"])
    lists_sum = attn_lists.astype(f32)
    for m in range(1, n_dp):
        pairs = [(source_of[d][m], d) for d in range(n_dp)]
        lists_sum = lists_sum + lax.ppermute(attn_lists, "dp", pairs).astype(f32)
    lists_sum = lists_sum.astype(bf16)
    first = jnp.where(g == 0, lists_sum[:, :q_half], lists_sum[:, q_half:])
    second = jnp.where(g == 0, lists_sum[:, q_half:], lists_sum[:, :q_half])
    plane = dot(jnp.concatenate([first, second], axis=1), w_out).astype(bf16)
    plane = plane.astype(f32) + lax.ppermute(plane, "tp", core).astype(f32)
    plane16 = plane.astype(bf16)
    crossed = lax.ppermute(plane16, "tp", across)
    sent_b, kept_b, came_b = project_pair(
        project_kernel, share, after(attn, block_a[0]), *both("o1"), *both("a3"), *both("b3")
    )
    plane = after(plane, sent_b)
    plane = plane + crossed.astype(f32)
    plane = (jnp.where(t == z, plane, 0.0) + hidden_lists).astype(bf16)
    vec_lists = dot(plane, w_pool).astype(bf16)
    lists_own, cols = centroids.shape
    late = vec_lists.reshape(n_dp, lists_own, n_tp, cols).transpose(0, 2, 1, 3)
    late = jnp.concatenate(
        [
            late,
            jnp.broadcast_to(
                local_counts.astype(bf16).reshape(n_dp, 1, lists_own, 1),
                (n_dp, n_tp, lists_own, HD),
            ),
        ],
        axis=3,
    ).reshape(n_dp * n_tp, lists_own, cols + HD)
    block_b = exchange(kept_b, after(came_b, vec_lists, block_a[1]), 1)
    late = lax.all_to_all(after(late, block_b[0]), ("dp", "tp"), split_axis=0, concat_axis=0, tiled=True)
    late = late.reshape(n_dp, n_tp, lists_own, cols + HD).astype(f32)
    totals = jnp.sum(late[..., :cols], axis=(0, 1))
    counts = jnp.sum(late[:, 0, :, cols], axis=0)
    residual_sums = totals - counts[:, None] * centroids
    list_counts = counts.astype(jnp.int32)
    (layer_out,) = call(
        finish_kernel,
        [shape((tokens, share), bf16)],
        tokens * share,
        scalars,
        own_input,
        *block_a,
        *block_b,
        vmem=TAIL,
    )
    return (layer_out, residual_sums, list_counts)


def solution(mesh):
    sizes = mesh.shape
    square = sizes["groups"] == 2 and sizes["dp"] == 4 and sizes["tp"] == 4
    return jax.shard_map(
        shards if square else wide_slice_shards,
        mesh=mesh,
        in_specs=(
            P(("groups", "dp"), None),
            P(("groups", "dp"), None),
            P(("groups", "dp"), None),
            P("groups"),
            P(),
            P("dp", "tp"),
            P("tp"),
            P("dp", "tp"),
            P(),
            P("tp", "dp"),
            P("tp", None),
            P("dp", "tp"),
        ),
        out_specs=(P(("groups", "dp"), "tp"), P(("groups", "dp"), "tp"), P(("groups", "dp"))),
        check_vma=False,
    )
```

```python
import functools

import jax
import jax.numpy as jnp
import numpy as np
from jax import lax
from jax.experimental import pallas as pl
from jax.experimental.pallas import tpu as pltpu
from jax.sharding import PartitionSpec as P

KV_HEADS = 4
HD = 128
Q_HEADS = 16


rope_base = 1000000.0
bf16 = jnp.bfloat16
f32 = jnp.float32


def rotate(values, places):
    half = HD // 2
    freq = rope_base ** (-(2.0 / HD) * jnp.arange(half, dtype=jnp.float32))
    angle = places.astype(jnp.float32)[:, None] * freq[None, :]
    cosine = jnp.cos(angle)[:, None, :]
    sine = jnp.sin(angle)[:, None, :]
    shaped = values.reshape(values.shape[0], -1, HD)
    first = shaped[..., :half]
    second = shaped[..., half:]
    turned = jnp.concatenate(
        [first * cosine - second * sine, second * cosine + first * sine], axis=-1
    )
    return turned.reshape(values.shape)


def positions_of(lengths_row, token_count, caption_count):
    ends = jnp.cumsum(lengths_row, dtype=jnp.int32)
    index = jnp.arange(token_count, dtype=jnp.int32)
    segment = jnp.sum((index[:, None] >= ends[None, :]).astype(jnp.int32), axis=1, dtype=jnp.int32)
    member = segment[None, :] == jnp.arange(caption_count, dtype=jnp.int32)[:, None]
    starts = ends - lengths_row
    place = index - jnp.sum(jnp.where(member, starts[:, None], 0), axis=0, dtype=jnp.int32)
    return (segment, member, place)


def wide_slice_shards(
    hidden,
    lengths,
    list_ids,
    list_slot,
    gain,
    w_query,
    b_query,
    w_keyval,
    b_keyval,
    w_out,
    w_pool,
    centroids,
):
    token_count = hidden.shape[0]
    caption_count = lengths.shape[1]
    dp_count = lax.axis_size("dp")
    tp_index = lax.axis_index("tp")
    wide = hidden.astype(jnp.float32)
    normed = (wide * lax.rsqrt(jnp.mean(wide * wide, axis=1, keepdims=True) + 1e-06) * gain).astype(
        jnp.bfloat16
    )
    segment, member, place = positions_of(lengths[0], token_count, caption_count)
    query_cols = w_query.shape[1]
    kv_width = b_keyval.shape[0] // 2
    head_group = tp_index * (query_cols // HD) // (Q_HEADS // KV_HEADS)
    full_cols = lax.all_gather(w_keyval, "tp", axis=1, tiled=True)
    query_sum = jnp.dot(
        normed,
        lax.all_gather(w_query, "dp", axis=0, tiled=True),
        preferred_element_type=jnp.float32,
    )
    own_cols = jnp.concatenate(
        [
            lax.dynamic_slice_in_dim(full_cols, head_group * HD, HD, 1),
            lax.dynamic_slice_in_dim(full_cols, kv_width + head_group * HD, HD, 1),
        ],
        axis=1,
    )
    keyval_sum = jnp.dot(
        normed,
        lax.all_gather(own_cols, "dp", axis=0, tiled=True),
        preferred_element_type=jnp.float32,
    )
    key_bias = lax.dynamic_slice_in_dim(b_keyval, head_group * HD, HD, 0)
    value_bias = lax.dynamic_slice_in_dim(b_keyval, kv_width + head_group * HD, HD, 0)
    keys = rotate(keyval_sum[:, :HD] + key_bias.astype(jnp.float32), place).astype(jnp.bfloat16)
    values = (keyval_sum[:, HD:] + value_bias.astype(jnp.float32)).astype(jnp.bfloat16)
    query = rotate(query_sum + b_query.astype(jnp.float32), place).astype(jnp.bfloat16)
    grouped = query.reshape(token_count, query_cols // HD, HD)
    scores = jnp.einsum("sgd,td->gst", grouped, keys, preferred_element_type=jnp.float32) * HD ** (
        -0.5
    )
    allowed = segment[:, None] == segment[None, :]
    scores = jnp.where(allowed[None], scores, -1e30)
    probs = jax.nn.softmax(scores, axis=-1).astype(jnp.bfloat16)
    attn = jnp.einsum("gst,td->sgd", probs, values, preferred_element_type=jnp.float32)
    attn = attn.astype(jnp.bfloat16).reshape(token_count, query_cols)
    partial_out = jnp.dot(
        attn, lax.all_gather(w_out, "dp", axis=1, tiled=True), preferred_element_type=jnp.float32
    )
    summed = lax.psum_scatter(
        partial_out.astype(jnp.bfloat16), "tp", scatter_dimension=1, tiled=True
    ).astype(jnp.float32)
    feature_share = summed.shape[1]
    own_input = lax.dynamic_slice_in_dim(wide, tp_index * feature_share, feature_share, 1)
    layer_out = (own_input + summed).astype(jnp.bfloat16)
    pooled = jnp.dot(member.astype(jnp.bfloat16), layer_out, preferred_element_type=jnp.float32)
    pooled = (pooled / lengths[0].astype(jnp.float32)[:, None]).astype(jnp.bfloat16)
    pooled_part = jnp.dot(pooled, w_pool, preferred_element_type=jnp.float32)
    vec = lax.psum_scatter(pooled_part.astype(jnp.bfloat16), "tp", scatter_dimension=1, tiled=True)
    lists_total = list_slot.shape[0]
    caption_lists = list_ids.reshape(-1)
    slot = jnp.sum(
        jnp.where(
            caption_lists[:, None] == jnp.arange(lists_total, dtype=jnp.int32)[None, :],
            list_slot[None, :],
            0,
        ),
        axis=1,
        dtype=jnp.int32,
    )
    lists_own = centroids.shape[0]
    send_cap = max(2, 2 * caption_count // dp_count)
    owner = slot // lists_own
    local = slot % lists_own
    order = jnp.arange(caption_count, dtype=jnp.int32)
    earlier = (owner[None, :] == owner[:, None]) & (order[None, :] < order[:, None])
    rank = jnp.sum(earlier.astype(jnp.int32), axis=1, dtype=jnp.int32)
    target = owner * send_cap + rank
    placed = jnp.arange(dp_count * send_cap, dtype=jnp.int32)[:, None] == target[None, :]
    send_values = jnp.dot(
        placed.astype(jnp.bfloat16), vec, preferred_element_type=jnp.float32
    ).astype(jnp.bfloat16)
    send_values = send_values.reshape(dp_count, send_cap, vec.shape[1])
    send_rows = jnp.sum(jnp.where(placed, local[None, :] + 1, 0), axis=1, dtype=jnp.int32).reshape(
        dp_count, send_cap
    )
    got_values, got_rows = (
        lax.all_to_all(send_values, "dp", split_axis=0, concat_axis=0, tiled=True),
        lax.all_to_all(send_rows, "dp", split_axis=0, concat_axis=0, tiled=True),
    )
    got_values = got_values.reshape(dp_count * send_cap, vec.shape[1])
    got_rows = got_rows.reshape(dp_count * send_cap)
    hits = got_rows[None, :] - 1 == jnp.arange(lists_own, dtype=jnp.int32)[:, None]
    totals = jnp.dot(hits.astype(jnp.bfloat16), got_values, preferred_element_type=jnp.float32)
    list_counts = jnp.sum(hits.astype(jnp.int32), axis=1, dtype=jnp.int32)
    residual_sums = totals - list_counts.astype(jnp.float32)[:, None] * centroids
    return (layer_out, residual_sums, list_counts)


VMEM = pl.BlockSpec(memory_space=pltpu.VMEM)
SMEM = pl.BlockSpec(memory_space=pltpu.SMEM)
T, GROUP, KEEP_0, KEEP_1, MINE_A, KEY_FROM, VALUE_FROM, SEND_1, SEND_2 = range(4, 13)
TAIL = 60


def dot(a, b):
    return jnp.dot(a, b, preferred_element_type=f32)


def turn(x, cosine, sine):
    return x * cosine + pltpu.roll(x, HD // 2, 1) * sine


def lanes(start, size):
    return pl.ds(pl.multiple_of(start, 128), size)


def call(kernel, outs, flops, scalars, *args, vmem=60):
    moved = sum(a.size * a.dtype.itemsize for a in (*args, *outs))
    return pl.pallas_call(
        kernel,
        in_specs=[SMEM] + [VMEM] * len(args),
        out_specs=[VMEM] * len(outs),
        out_shape=outs,
        compiler_params=pltpu.CompilerParams(vmem_limit_bytes=vmem * 1024 * 1024),
        cost_estimate=pl.CostEstimate(flops=flops, bytes_accessed=moved, transcendentals=0),
    )(scalars, *args)


def places_kernel(
    freq, lengths, ids, slots, cos_ref, sin_ref, seg_col, seg_row, member_ref, inverse_ref, hits_ref, counts_ref
):
    i32 = jnp.int32
    tokens = cos_ref.shape[0]
    captions = lengths.shape[1]
    lists = slots.shape[1]
    row = lengths[...]
    square = (captions, captions)
    down = lax.broadcasted_iota(i32, square, 0)
    along = lax.broadcasted_iota(i32, square, 1)
    wide_row = jnp.broadcast_to(row, square)
    col = jnp.sum(jnp.where(down == along, wide_row, 0), axis=1, keepdims=True)
    end_col = jnp.sum(jnp.where(along <= down, wide_row, 0), axis=1, keepdims=True)
    start_col = end_col - col
    end_row = jnp.sum(jnp.where(down <= along, jnp.broadcast_to(col, square), 0), axis=0, keepdims=True)
    start_row = end_row - row
    inverse_ref[...] = 1.0 / col.astype(f32)
    index = lax.broadcasted_iota(i32, (captions, tokens), 1)
    member_ref[...] = jnp.where((index >= start_col) & (index < end_col), 1.0, 0.0).astype(bf16)
    seg_row[...] = jnp.sum(jnp.where(index >= end_col, 1, 0), axis=0, keepdims=True)
    index = lax.broadcasted_iota(i32, (tokens, captions), 0)
    seg_col[...] = jnp.sum(jnp.where(index >= end_row, 1, 0), axis=1, keepdims=True)
    inside = (index >= start_row) & (index < end_row)
    place = jnp.sum(jnp.where(inside, index - start_row, 0), axis=1, keepdims=True)
    angle = place.astype(f32) * freq[...]
    cos_ref[...] = jnp.cos(angle)
    sine = jnp.sin(angle)
    lane = lax.broadcasted_iota(i32, (tokens, HD), 1)
    sin_ref[...] = jnp.where(lane < HD // 2, -sine, sine)
    square = (lists, lists)
    down = lax.broadcasted_iota(i32, square, 0)
    along = lax.broadcasted_iota(i32, square, 1)
    slot_col = jnp.sum(
        jnp.where(down == along, jnp.broadcast_to(slots[...], square), 0), axis=1, keepdims=True
    )
    down = lax.broadcasted_iota(i32, (lists, captions), 0)
    slot_row = jnp.sum(jnp.where(ids[...] == down, slot_col, 0), axis=0, keepdims=True)
    hits = jnp.where(down == slot_row, 1.0, 0.0)
    hits_ref[...] = hits.astype(bf16)
    counts_ref[...] = jnp.sum(hits, axis=1, keepdims=True)


def places(lengths, list_ids, list_slot, tokens):
    captions, lists = lengths.shape[1], list_slot.shape[0]
    freq = rope_base ** (-(2.0 / HD) * (np.arange(HD) % (HD // 2)))
    shape = jax.ShapeDtypeStruct
    return pl.pallas_call(
        places_kernel,
        in_specs=[VMEM] * 4,
        out_specs=[VMEM] * 8,
        out_shape=[
            shape((tokens, HD), f32),
            shape((tokens, HD), f32),
            shape((tokens, 1), jnp.int32),
            shape((1, tokens), jnp.int32),
            shape((captions, tokens), bf16),
            shape((captions, 1), f32),
            shape((lists, captions), bf16),
            shape((lists, 1), f32),
        ],
        compiler_params=pltpu.CompilerParams(vmem_limit_bytes=60 * 1024 * 1024),
        cost_estimate=pl.CostEstimate(
            flops=64 * tokens * HD, bytes_accessed=tokens * HD * 8, transcendentals=2 * tokens * HD
        ),
    )(jnp.asarray(freq, f32)[None, :], lengths, list_ids, list_slot[None, :])


def prep_kernel(sc, hidden_ref, gain_ref, member_ref, *outs):
    *block_refs, own_ref, pooled_ref = outs
    wide = hidden_ref[...].astype(f32)
    scale = lax.rsqrt(jnp.mean(wide * wide, axis=1, keepdims=True) + 1e-06)
    share = own_ref.shape[1]
    for m, ref in enumerate(block_refs):
        at = lanes(sc[m] * share, share)
        ref[...] = (hidden_ref[:, at].astype(f32) * scale * gain_ref[:, at]).astype(bf16)
    own = hidden_ref[:, lanes(sc[T] * share, share)]
    own_ref[...] = own

    @pl.when(pl.program_id(0) == 0)
    def _():
        pooled_ref[...] = jnp.zeros_like(pooled_ref)

    pooled_ref[...] += dot(member_ref[...], own)


def prepare(scalars, hidden, gain, member, n):
    tokens, width = hidden.shape
    share = width // n
    captions = member.shape[0]
    rows = 128
    stripe = pl.BlockSpec((rows, share), lambda i, s: (i, 0))
    return pl.pallas_call(
        prep_kernel,
        grid_spec=pltpu.PrefetchScalarGridSpec(
            num_scalar_prefetch=1,
            grid=(tokens // rows,),
            in_specs=[
                pl.BlockSpec((rows, width), lambda i, s: (i, 0)),
                pl.BlockSpec((1, width), lambda i, s: (0, 0)),
                pl.BlockSpec((captions, rows), lambda i, s: (0, i)),
            ],
            out_specs=[stripe] * (n + 1) + [pl.BlockSpec((captions, share), lambda i, s: (0, 0))],
        ),
        out_shape=[jax.ShapeDtypeStruct((tokens, share), bf16)] * (n + 1)
        + [jax.ShapeDtypeStruct((captions, share), f32)],
        compiler_params=pltpu.CompilerParams(vmem_limit_bytes=60 * 1024 * 1024),
        cost_estimate=pl.CostEstimate(
            flops=8 * tokens * width, bytes_accessed=4 * tokens * width, transcendentals=0
        ),
    )(scalars, hidden, gain[None, :], member)


def projection_kernel(sc, b0, b1, b2, b3, wk, wq, r1, r2, r3, y1, y3, kv_ref, own_ref, oth_ref):
    g = sc[GROUP]
    half = own_ref.shape[1]
    own = dot(b1[...], r1[...]) + dot(b2[...], r2[...]) + dot(b3[...], r3[...])
    oth = dot(b1[...], y1[...]) + dot(b3[...], y3[...])
    base = dot(b0[...], wk[...])
    for h in range(wk.shape[1] // HD):
        at = slice(h * HD, (h + 1) * HD)
        kv_ref[:, at] = base[:, at] + jnp.where(g == h, own[:, :HD], oth[:, :HD])
    own_ref[...] = own[:, HD:] + dot(b0[...], wq[:, lanes(g * half, half)])
    oth_ref[...] = oth[:, HD:] + dot(b0[...], wq[:, lanes((1 - g) * half, half)])


def keyval_kernel(sc, kv_ref, b2, y2, bias, cos_ref, sin_ref, out_ref, send_1, send_2):
    g, t = sc[GROUP], sc[T]
    last = dot(b2[...], y2[:, :HD])
    heads = kv_ref.shape[1] // HD
    keyed = t * heads < KV_HEADS
    for h in range(heads):
        at = slice(h * HD, (h + 1) * HD)
        x = kv_ref[:, at] + jnp.where(g == h, 0.0, last)
        x = x + bias[:, lanes((t * heads + h) * HD, HD)].astype(f32)
        out_ref[:, at] = jnp.where(keyed, turn(x, cos_ref[...], sin_ref[...]), x).astype(bf16)
    send_1[...] = out_ref[:, lanes(sc[SEND_1] * HD, HD)]
    send_2[...] = out_ref[:, lanes(sc[SEND_2] * HD, HD)]


def attention_kernel(
    sc,
    own_ref,
    oth_ref,
    b2,
    y2,
    bq_ref,
    x0,
    x1,
    x2,
    cos_ref,
    sin_ref,
    seg_col,
    seg_row,
    member_ref,
    inverse_ref,
    hits_ref,
    out_ref,
    lists_ref,
    query_ref,
):
    t, g = sc[T], sc[GROUP]
    tokens, wide = own_ref.shape
    heads = wide // HD
    here = lanes((t % (x0.shape[1] // HD)) * HD, HD)

    def pick(origin):
        return jnp.where(
            origin == 0, x0[:, here], jnp.where(origin == 1, x1[...], x2[...])
        )

    keys, values = pick(sc[KEY_FROM]), pick(sc[VALUE_FROM])
    query_ref[...] = oth_ref[...] + dot(b2[...], y2[:, HD:])
    rows = 128
    pooled = jnp.zeros((member_ref.shape[0], 2 * wide), f32)
    for i in range(tokens // rows):
        at = pl.ds(i * rows, rows)
        lo_key, hi_key = max(0, (i - 1) * rows), min(tokens, (i + 2) * rows)
        cosine, sine = cos_ref[at, :], sin_ref[at, :]
        allowed = seg_col[at, :] == seg_row[:, lo_key:hi_key]
        out = []
        for part, ref in enumerate((own_ref, query_ref)):
            for h in range(heads):
                lo = h * HD
                bias = bq_ref[:, lanes(jnp.bitwise_xor(g, part) * wide + lo, HD)].astype(f32)
                query = turn(ref[at, lo : lo + HD] + bias, cosine, sine).astype(bf16)
                scores = lax.dot_general(
                    query,
                    keys[lo_key:hi_key],
                    (((1,), (1,)), ((), ())),
                    preferred_element_type=f32,
                ) * HD ** (-0.5)
                scores = jnp.where(allowed, scores, -1e30)
                top = jnp.max(scores, axis=1, keepdims=True)
                weights = jnp.exp(scores - top)
                probs = (weights / jnp.sum(weights, axis=1, keepdims=True)).astype(bf16)
                out.append(dot(probs, values[lo_key:hi_key]).astype(bf16))
        out = jnp.concatenate(out, axis=1)
        out_ref[at, :] = out
        pooled = pooled + dot(member_ref[:, at], out)
    pooled = (pooled * inverse_ref[...]).astype(bf16)
    lists_ref[...] = dot(hits_ref[...], pooled).astype(bf16)


def attend(scalars, own, *rest):
    tokens, wide = own.shape
    lists = rest[-1].shape[0]
    outs = [
        jax.ShapeDtypeStruct((tokens, 2 * wide), bf16),
        jax.ShapeDtypeStruct((lists, 2 * wide), bf16),
    ]
    return pl.pallas_call(
        attention_kernel,
        in_specs=[SMEM] + [VMEM] * (1 + len(rest)),
        out_specs=[VMEM] * 2,
        out_shape=outs,
        scratch_shapes=[pltpu.VMEM((tokens, wide), f32)],
        compiler_params=pltpu.CompilerParams(vmem_limit_bytes=60 * 1024 * 1024),
        cost_estimate=pl.CostEstimate(
            flops=8 * tokens * tokens * wide,
            bytes_accessed=8 * 1024 * 1024,
            transcendentals=tokens * tokens * 2 * wide // HD,
        ),
    )(scalars, own, *rest)


def project(attn, weights, ref):
    half = attn.shape[1] // 2
    left, right = attn[:, :half], attn[:, half:]
    lo = 0
    for first, second in weights():
        hi = lo + first.shape[1]
        ref[:, lo:hi] = (dot(left, first) + dot(right, second)).astype(bf16)
        lo = hi


def project_two(keep, attn, first, second, sent, kept):
    @pl.when(keep == 1)
    def _():
        project(attn, first, kept)
        project(attn, second, sent)

    @pl.when(keep == 0)
    def _():
        project(attn, second, kept)
        project(attn, first, sent)


def project_own_kernel(sc, attn, lists, w, own_b, oth_b, sent, kept, list_sent, list_kept):
    half = attn.shape[1] // 2
    g = sc[GROUP]

    def stored():
        return [
            (
                w[pl.ds(pl.multiple_of(g * half, half), half), :],
                w[pl.ds(pl.multiple_of((1 - g) * half, half), half), :],
            )
        ]

    second = lambda: [(own_b[...], oth_b[...])]
    project_two(sc[KEEP_0], attn, stored, second, sent, kept)
    project_two(sc[KEEP_0], lists, stored, second, list_sent, list_kept)


def project_kernel(
    sc, attn, lists, own_a, oth_a, own_b, oth_b, own_c, oth_c, sent, kept, list_sent, list_kept
):
    first = lambda: [(own_a[...], oth_a[...])]
    second = lambda: [(own_b[...], oth_b[...]), (own_c[...], oth_c[...])]
    project_two(sc[KEEP_1], attn, first, second, sent, kept)
    project_two(sc[KEEP_1], lists, first, second, list_sent, list_kept)


def add_kernel(sc, kept, came, total):
    total[...] = (kept[...].astype(f32) + came[...].astype(f32)).astype(bf16)


def finish_kernel(sc, own, ta, ca, tb, cb, out):
    @pl.when(sc[MINE_A] == 1)
    def _():
        out[...] = (own[...].astype(f32) + (ta[...].astype(f32) + ca[...].astype(f32))).astype(bf16)

    @pl.when(sc[MINE_A] == 0)
    def _():
        out[...] = (own[...].astype(f32) + (tb[...].astype(f32) + cb[...].astype(f32))).astype(bf16)


def folded_ring(n):
    return [0] + list(range(1, n, 2)) + list(range(2 * ((n - 1) // 2), 0, -2))


def after(value, *earlier):
    return lax.optimization_barrier((value, *earlier))[0]


def shards(
    hidden,
    lengths,
    list_ids,
    list_slot,
    gain,
    w_query,
    b_query,
    w_keyval,
    b_keyval,
    w_out,
    w_pool,
    centroids,
):
    tokens, width = hidden.shape
    captions = lengths.shape[1]
    n_dp, n_tp = lax.axis_size("dp"), lax.axis_size("tp")
    share = width // n_dp
    ring = folded_ring(n_dp)
    place_in = {v: i for i, v in enumerate(ring)}
    source_of = [[ring[(place_in[d] - m) % n_dp] for m in range(n_dp)] for d in range(n_dp)]
    forward = [(ring[i], ring[(i + 1) % n_dp]) for i in range(n_dp)]
    backward = [(b, a) for a, b in forward]
    swap = [(0, 1), (1, 0)]
    core = [(i, i ^ 1) for i in range(n_tp)]
    across = [(i, i ^ 2) for i in range(n_tp)]
    per_dev = w_keyval.shape[1] // HD
    rounds = [[], []]
    sends = [[0] * n_tp, [0] * n_tp]
    origin = []
    for tt in range(n_tp):
        for head in (tt, KV_HEADS + tt):
            source = head // per_dev
            if source == tt:
                origin.append(0)
                continue
            for k, pairs in enumerate(rounds):
                if all(a != source and b != tt for a, b in pairs):
                    pairs.append((source, tt))
                    sends[k][source] = head % per_dev
                    origin.append(k + 1)
                    break
    table = []
    for gg in range(2):
        for d in range(n_dp):
            for tt in range(n_tp):
                stays = [int(source_of[d][m] % 2 == tt % 2) for m in range(2)]
                mine = int(tt in (source_of[d][0], source_of[d][2]))
                table.append(
                    [*source_of[d], tt, gg, *stays, mine, *origin[2 * tt : 2 * tt + 2], sends[0][tt], sends[1][tt]]
                )
    scalars = lax.dynamic_slice_in_dim(
        jnp.array(table, jnp.int32),
        lax.axis_index(("groups", "dp", "tp")),
        1,
        0,
        allow_negative_indices=False,
    )[0]
    g, t, z = lax.axis_index("groups"), lax.axis_index("tp"), lax.axis_index("dp")

    def own_half(w, axis):
        size = w.shape[axis] // 2
        return lax.dynamic_slice_in_dim(w, g * size, size, axis, allow_negative_indices=False)

    cosine, sine, seg_col, seg_row, member, inverse, hits, local_counts = places(
        lengths, list_ids, list_slot, tokens
    )

    kq_own = jnp.concatenate([own_half(w_keyval, 1), own_half(w_query, 1)], axis=1)
    o_own = own_half(w_out, 0)
    cut = share // 256 * 128 + 128

    own = {"q": kq_own, "o": o_own, "a": o_own[:, :cut], "b": o_own[:, cut:]}
    stages = [["q1"], ["q3"], ["q2"], ["o1", "a3"], ["o2", "b3"]]
    lag = 2
    ring_of, swapped = {}, {}

    def run_stage(i, *ties, swap_ties=()):
        ties = list(ties)
        if i >= 1:
            ties += [ring_of[key] for key in stages[i - 1]]
        if i >= lag:
            ties += [swapped[key] for key in stages[i - lag]]
        for key in stages[i]:
            piece = ring_of[key[0] + "1"] if key[1] == "2" else own[key[0]]
            pairs = backward if key[1] == "3" else forward
            ring_of[key] = lax.ppermute(after(piece, *ties) if ties else piece, "dp", pairs)
        for key in stages[i]:
            came = ring_of[key]
            if swap_ties:
                came = after(came, *swap_ties, *[ring_of[k] for k in stages[i]])
            swapped[key] = lax.ppermute(came, "groups", swap)

    run_stage(0)
    *blocks, own_input, pooled_hidden = prepare(scalars, hidden, gain, member, n_dp)
    run_stage(1, blocks[0], cosine)
    run_stage(2)
    run_stage(3)
    hidden_lists = dot(hits, (pooled_hidden * inverse).astype(bf16))

    shape = jax.ShapeDtypeStruct
    work = 2 * tokens * width
    q_half = w_query.shape[1] // 2
    kv_sum, sum_own, sum_oth = call(
        projection_kernel,
        [shape((tokens, w_keyval.shape[1]), f32)] + [shape((tokens, q_half), f32)] * 2,
        work * (q_half * 2 + w_keyval.shape[1]),
        scalars,
        *blocks,
        w_keyval,
        w_query,
        *[ring_of[key] for key in ("q1", "q2", "q3")],
        *[swapped[key] for key in ("q1", "q3")],
    )
    kv_mine, *kv_sent = call(
        keyval_kernel,
        [shape(kv_sum.shape, bf16)] + [shape((tokens, HD), bf16)] * 2,
        tokens * share * HD,
        scalars,
        kv_sum,
        blocks[2],
        swapped["q2"],
        b_keyval[None, :],
        cosine,
        sine,
    )
    kv_came = [lax.ppermute(x, "tp", pairs) for x, pairs in zip(kv_sent, rounds)]
    run_stage(4, sum_own, swap_ties=[*kv_came, swapped["o1"], swapped["a3"]])
    attn, attn_lists = attend(
        scalars,
        after(sum_own, ring_of["b3"], ring_of["o2"]),
        sum_oth,
        blocks[2],
        swapped["q2"],
        b_query[None, :],
        kv_mine,
        *kv_came,
        cosine,
        sine,
        seg_col,
        seg_row,
        member,
        inverse,
        hits,
    )

    def project_pair(kernel, n, attn, *weights):
        sent, kept, *lists = call(
            kernel,
            [shape((tokens, n), bf16)] * 2 + [shape((attn_lists.shape[0], n), bf16)] * 2,
            4 * tokens * q_half * 2 * n,
            scalars,
            attn,
            attn_lists,
            *weights,
            vmem=TAIL,
        )
        return sent, kept, lax.ppermute(sent, "tp", core), lists

    def exchange(kept, came, m):
        (total,) = call(
            add_kernel, [shape(kept.shape, bf16)], kept.size, scalars, kept, came, vmem=TAIL
        )
        pairs = []
        for d in range(n_dp):
            for block in (source_of[d][m], source_of[d][m + 2]):
                pairs.append((d * n_tp + (block ^ 2), d * n_tp + block))
        return total, lax.ppermute(total, ("dp", "tp"), pairs)

    def both(key):
        return ring_of[key], swapped[key]

    sent_a, kept_a, came_a, lists_a = project_pair(project_own_kernel, share, attn, w_out, *both("o2"))
    block_a = exchange(kept_a, came_a, 0)

    sent_b, kept_b, came_b, lists_b = project_pair(
        project_kernel, share, after(attn, sent_a), *both("o1"), *both("a3"), *both("b3")
    )

    count = attn_lists.shape[0]
    mine_a = scalars[MINE_A] == 1
    list_came = lax.ppermute(jnp.concatenate([lists_a[0], lists_b[0]], axis=0), "tp", core)
    list_a = lists_a[1].astype(f32) + list_came[:count].astype(f32)
    list_b = lists_b[1].astype(f32) + list_came[count:].astype(f32)
    list_give = jnp.where(mine_a, list_b, list_a).astype(bf16)
    list_got = lax.ppermute(after(list_give, block_a[0]), "tp", across).astype(f32)
    plane = jnp.where(mine_a, list_a, list_b) + list_got + hidden_lists
    vec_lists = dot(plane.astype(bf16), w_pool).astype(bf16)
    lists_own, cols = centroids.shape
    late = vec_lists.reshape(n_dp, lists_own, n_tp, cols).transpose(0, 2, 1, 3)
    late = jnp.concatenate(
        [
            late,
            jnp.broadcast_to(
                local_counts.astype(bf16).reshape(n_dp, 1, lists_own, 1),
                (n_dp, n_tp, lists_own, HD),
            ),
        ],
        axis=3,
    ).reshape(n_dp * n_tp, lists_own, cols + HD)
    block_b = exchange(kept_b, after(came_b, block_a[0]), 1)
    late = lax.all_to_all(after(late, block_b[0]), ("dp", "tp"), split_axis=0, concat_axis=0, tiled=True)
    late = late.reshape(n_dp, n_tp, lists_own, cols + HD).astype(f32)
    totals = jnp.sum(late[..., :cols], axis=(0, 1))
    counts = jnp.sum(late[:, 0, :, cols], axis=0)
    residual_sums = totals - counts[:, None] * centroids
    list_counts = counts.astype(jnp.int32)
    (layer_out,) = call(
        finish_kernel,
        [shape((tokens, share), bf16)],
        tokens * share,
        scalars,
        own_input,
        *block_a,
        *block_b,
        vmem=TAIL,
    )
    return (layer_out, residual_sums, list_counts)


def solution(mesh):
    sizes = mesh.shape
    square = sizes["groups"] == 2 and sizes["dp"] == 4 and sizes["tp"] == 4
    return jax.shard_map(
        shards if square else wide_slice_shards,
        mesh=mesh,
        in_specs=(
            P(("groups", "dp"), None),
            P(("groups", "dp"), None),
            P(("groups", "dp"), None),
            P("groups"),
            P(),
            P("dp", "tp"),
            P("tp"),
            P("dp", "tp"),
            P(),
            P("tp", "dp"),
            P("tp", None),
            P("dp", "tp"),
        ),
        out_specs=(P(("groups", "dp"), "tp"), P(("groups", "dp"), "tp"), P(("groups", "dp"))),
        check_vma=False,
    )
```
